512 devices in a mesh: slab: 16 (over y, core), col: 32 (over x, z).
Axes of the slice: x: 4, y: 8, z: 8, core: 2. Of those that a mesh axis runs over, the one named last changes fastest.
Arguments:
- load: float32 [3, 256, 512, 128], P(None, 'slab', 'col'), may hold values from -6 to 6
- density: int32 [256, 512, 128], P('slab', 'col'), may hold values from 0 to 7
- moduli: float32 [8], replicated, may hold values from 0.1 to 10
- fixed: int32 [256, 512, 128], P('slab', 'col'), may hold values 0 or 1
Outputs:
- solution_field: float32 [3, 256, 512, 128], P(None, 'slab', 'col')
- residual: float32 [3, 256, 512, 128], P(None, 'slab', 'col')
The draws below stay inside these ranges and needn't reach their ends.
All inputs are finite; a program needn't handle non-finite values. No bound on the sum of `fixed` on one device may be relied on, other than what follows from the above.
Results may differ from the reference program's by a relative error of at most 0.0001.
Values sent between devices are 32-bit elements; how exact they have to be, the bound alone decides.
No kernel may reach another device: no remote copies, remote signals or barrier semaphores. Data moves between devices by JAX's collectives and lax.ppermute only.
A program may use at most 128 MiB of HBM per device.

```python
import math
import jax
import jax.numpy as jnp

NX = 128
LEVELS = 3
PRE = 2
POST = 2
COARSE_SWEEPS = 8
CLASSES = 8
NZ = 256
NY = 512


def set_ends(array, rng, least, high):
    place = [jax.random.randint(jax.random.fold_in(rng, axis), (), 0, length) for axis, length in enumerate(array.shape)]
    widest = array.shape.index(max(array.shape))
    neighbour = place[:widest] + [(place[widest] + 1) % array.shape[widest]] + place[widest + 1:]
    return array.at[tuple(place)].set(least).at[tuple(neighbour)].set(high)


def steps_of(own_key, dims, pieces, smallest, top_value):
    loudness = 1.0
    for dim, parts in pieces:
        heights = jax.random.uniform(jax.random.fold_in(jax.random.fold_in(own_key, 6), dim), (parts,), jnp.float32, smallest / len(pieces), top_value / len(pieces))
        loudness = loudness * jnp.repeat(jnp.exp(heights), dims[dim] // parts).reshape((-1,) + (1,) * (len(dims) - 1 - dim))
    return loudness


def centred(rng, shape, scale, bound, split=(), held_as=jnp.bfloat16):
    drawn = jax.random.normal(rng, shape, jnp.float32) * scale
    if len(split) > 0:
        drawn = steps_of(rng, shape, split, -0.22, 0.18) * drawn
    return jnp.clip(drawn, min=-bound, max=bound).astype(held_as)


def setup_inputs(seed: int = 0) -> dict:
    key_list = jax.random.split(jax.random.key(seed), 5)
    return {
        "load": centred(key_list[0], (3, NZ, NY, NX), 1.0, 6.0, ((1, 16), (2, 32)), jnp.float32),
        "density": set_ends(jax.random.randint(key_list[1], (NZ, NY, NX), 0, CLASSES), jax.random.fold_in(key_list[1], 1), 0, CLASSES - 1).astype(jnp.int32),
        "moduli": jnp.clip(jnp.exp(jax.random.uniform(key_list[2], (CLASSES,), jnp.float32, math.log(0.1), math.log(10.0))), 0.1, 10.0),
        "fixed": set_ends((jax.random.randint(key_list[3], (NZ, NY, NX), 0, 8) < 1).astype(jnp.int32), jax.random.fold_in(key_list[3], 1), 0, 1),
    }


OMEGA = 0.6
COUPLE = 0.05


def shrink(arr):
    lead = arr.shape[:-3]
    za, yb, xc = arr.shape[-3:]
    blocks = arr.reshape(tuple(lead) + (za // 2, 2, yb // 2, 2, xc // 2, 2))
    return blocks.mean(axis=(-5, -3, -1))


def grow(arr):
    return jnp.repeat(jnp.repeat(jnp.repeat(arr, 2, axis=-3), 2, axis=-2), 2, axis=-1)


def beside_all(padded):
    return [padded[..., 2:, 1:-1, 1:-1], padded[..., :-2, 1:-1, 1:-1],
            padded[..., 1:-1, 2:, 1:-1], padded[..., 1:-1, :-2, 1:-1],
            padded[..., 1:-1, 1:-1, 2:], padded[..., 1:-1, 1:-1, :-2]]


def diagonal_of(stiff_pad, scale):
    centre = stiff_pad[1:-1, 1:-1, 1:-1]
    total = jnp.zeros_like(centre)
    for near in beside_all(stiff_pad):
        total = total + 0.5 * (centre + near)
    return scale * total + 2.0 * COUPLE * centre


def apply_op(field_pad, stiff_pad, scale):
    centre = stiff_pad[1:-1, 1:-1, 1:-1]
    field = field_pad[:, 1:-1, 1:-1, 1:-1]
    total = jnp.zeros_like(field)
    for near_k, near_u in zip(beside_all(stiff_pad), beside_all(field_pad)):
        total = total + 0.5 * (centre + near_k) * (field - near_u)
    return scale * total + COUPLE * centre * (field + jnp.sum(field, axis=0, keepdims=True))


def pad_field(field):
    return jnp.pad(field, ((0, 0), (1, 1), (1, 1), (1, 1)))


def sweeps(field, rhs, stiff_pad, diag, scale, weight, count):
    if field is None:
        field = OMEGA * weight * rhs / diag
        count = count - 1
    for turn in range(count):
        field = field + OMEGA * weight * (rhs - apply_op(pad_field(field), stiff_pad, scale)) / diag
    return field


def reference(load, density, moduli, fixed):
    stiff = jnp.zeros(density.shape, jnp.float32)
    for klass in range(CLASSES):
        stiff = stiff + jnp.where(density == klass, moduli[klass], jnp.float32(0.0))
    mask = 1.0 - fixed.astype(jnp.float32)
    pads, diags = [], []
    for level in range(LEVELS + 1):
        padded = jnp.pad(stiff, 1)
        pads.append(padded)
        diags.append(diagonal_of(padded, 0.25 ** level))
        if level < LEVELS:
            stiff = shrink(stiff)
    saved = []
    rhs = load
    for level in range(LEVELS):
        weight = mask if level == 0 else 1.0
        scale = 0.25 ** level
        field = sweeps(None, rhs, pads[level], diags[level], scale, weight, PRE)
        resid = weight * (rhs - apply_op(pad_field(field), pads[level], scale))
        saved.append((field, rhs))
        rhs = shrink(resid)
    field = sweeps(None, rhs, pads[LEVELS], diags[LEVELS], 0.25 ** LEVELS, 1.0, COARSE_SWEEPS)
    for level in range(LEVELS - 1, -1, -1):
        weight = mask if level == 0 else 1.0
        fine, rhs = saved[level]
        field = fine + weight * grow(field)
        field = sweeps(field, rhs, pads[level], diags[level], 0.25 ** level, weight, POST)
    residual = mask * (load - apply_op(pad_field(field), pads[0], 1.0))
    return field, residual
```

```python
import functools

import jax
import jax.numpy as jnp
from jax import lax
from jax.experimental import pallas as pl
from jax.experimental.pallas import tpu as pltpu
from jax.sharding import PartitionSpec as P

CLASSES = 8
OMEGA = 0.6
COUPLE = 0.05
SLAB = 16
COL = 32
F32 = jnp.float32


def lanes_of(rows):
    return lax.broadcasted_iota(jnp.int32, (rows, 128), 1)


def lane_next(v, step):
    return pltpu.roll(v, 128 - step, 1)


def lane_prev(v, step):
    return pltpu.roll(v, step, 1)


def row_next(v):
    return pltpu.roll(v, v.shape[0] - 1, 0)


def row_prev(v):
    return pltpu.roll(v, 1, 0)


def spread(v, lane, width):
    step = 1
    while step < width:
        v = v + jnp.where((lane & step) != 0, lane_prev(v, step), lane_next(v, step))
        step *= 2
    return v


def coefficients(k, k_lo, k_hi, scale, step, mask, total=None):
    lane = lanes_of(k.shape[0])
    half = 0.5 * scale
    k_next = lane_next(k, step)
    cx = jnp.where(lane < 128 - step, half * (k + k_next), 0.0)
    ky = row_next(k)
    cy = half * (k + ky)
    cz = half * (k + k_hi)
    if total is None:
        sides = jnp.where(lane < 128 - step, k_next, 0.0) + jnp.where(lane >= step, lane_prev(k, step), 0.0)
        total = half * (6.0 * k + sides + ky + row_prev(k) + k_lo + k_hi)
    diag = total + 2.0 * COUPLE * k
    top = OMEGA if mask is None else OMEGA * mask
    weight = jnp.where(k > 0.0, top / diag, 0.0)
    return cx, cy, cz, total + COUPLE * k, weight


def remainder(b, u, u_lo, u_hi, k, cx, cy, cz, cz_lo, e, step):
    cx_lo = lane_prev(cx, step)
    cy_lo = row_prev(cy)
    shared = COUPLE * k * (u[0] + u[1] + u[2])
    out = []
    for c in range(3):
        v = u[c]
        around = cx * lane_next(v, step) + cx_lo * lane_prev(v, step)
        around = around + cy * row_next(v) + cy_lo * row_prev(v)
        around = around + cz * u_hi[c] + cz_lo * u_lo[c]
        out.append((b[c] - shared) + (around - e * v))
    return out


def fill_coefficients(k_ref, co, planes, scale, step, mask_ref=None, total_ref=None):
    cx_ref, cy_ref, cz_ref, e_ref, w_ref = co

    def body(p, carry):
        mask = None if mask_ref is None else mask_ref[p]
        total = None if total_ref is None else total_ref[p]
        cx, cy, cz, e, w = coefficients(k_ref[p], k_ref[p - 1], k_ref[p + 1], scale, step, mask, total)
        cx_ref[p] = cx
        cy_ref[p] = cy
        cz_ref[p] = cz
        e_ref[p] = e
        w_ref[p] = w
        return carry

    lax.fori_loop(planes[0], planes[1], body, 0)


def left_over(p, b_ref, u_ref, k_ref, co, step, rows=slice(None)):
    cx_ref, cy_ref, cz_ref, e_ref, _ = co
    b = [b_ref[c, p] for c in range(3)]
    u = [u_ref[c, p] for c in range(3)]
    lo = [u_ref[c, p - 1] for c in range(3)]
    hi = [u_ref[c, p + 1] for c in range(3)]
    return u, remainder(b, u, lo, hi, k_ref[p], cx_ref[p], cy_ref[p], cz_ref[p], cz_ref[p - 1], e_ref[p], step)


def sweep(planes, b_ref, u_ref, new_ref, k_ref, co, step):
    def body(p, carry):
        u, rest = left_over(p, b_ref, u_ref, k_ref, co, step)
        w = co[4][p]
        for c in range(3):
            new_ref[c, p] = u[c] + w * rest[c]
        return carry

    lax.fori_loop(planes[0], planes[1], body, 0)


def first_sweep(planes, b_ref, new_ref, w_ref):
    def body(p, carry):
        w = w_ref[p]
        for c in range(3):
            new_ref[c, p] = w * b_ref[c, p]
        return carry

    lax.fori_loop(planes[0], planes[1], body, 0)


def block_mean(a, b, tmp, step):
    lane = lanes_of(a.shape[0])
    s = a + b
    s = s + jnp.where((lane & step) != 0, lane_prev(s, step), lane_next(s, step))
    n = a.shape[0]
    tmp[0:n] = s
    return 0.125 * (tmp[pl.ds(0, n // 2, stride=2)] + tmp[pl.ds(1, n // 2, stride=2)])


def double_rows(v, tmp):
    n = v.shape[0]
    tmp[pl.ds(0, n, stride=2)] = v
    tmp[pl.ds(1, n, stride=2)] = v


def prep_kernel(moduli, load, density, fixed, k_out, m_out, low, high):
    for z in range(16):
        d = density[z]
        k = jnp.zeros((16, 128), F32)
        for klass in range(CLASSES):
            k = jnp.where(d == klass, moduli[klass], k)
        m = 1.0 - fixed[z].astype(F32)
        k_out[z] = k
        m_out[z] = m
        for c in range(3):
            low[z, 4 * c : 4 * c + 4] = load[c, z, 0:4]
            high[z, 4 * c : 4 * c + 4] = load[c, z, 12:16]
        low[z, 12:16] = m[0:4]
        high[z, 12:16] = m[12:16]
        low[z, 16:24] = k[0:8]
        high[z, 16:24] = k[8:16]


def planes_kernel(load, k, m, from_low, from_high, low, high):
    for out, start in ((low, 0), (high, 12)):
        for q in range(4):
            z = start + q
            for a in range(4):
                base = 24 * (4 * a + q)
                own = load[a, z] if a < 3 else m[z]
                out[base : base + 4] = from_low[z, 4 * a : 4 * a + 4]
                out[base + 4 : base + 20] = own
                out[base + 20 : base + 24] = from_high[z, 4 * a : 4 * a + 4]
        for q in range(5):
            z = q if start == 0 else 11 + q
            base = 384 + 32 * q
            out[base : base + 8] = from_low[z, 16:24]
            out[base + 8 : base + 24] = k[z]
            out[base + 24 : base + 32] = from_high[z, 16:24]


def fine_kernel(load, k_own, m_own, y_low, y_high, z_low, z_high,
                b, u, k, m, message,
                cx, cy, cz, e, w, first, k1, tmp):
    co = (cx, cy, cz, e, w)
    for z in range(16):
        p = z + 5
        for c in range(3):
            b[c, p, 4:8] = y_low[z, 4 * c : 4 * c + 4]
            b[c, p, 8:24] = load[c, z]
            b[c, p, 24:28] = y_high[z, 4 * c : 4 * c + 4]
        m[p, 4:8] = y_low[z, 12:16]
        m[p, 8:24] = m_own[z]
        m[p, 24:28] = y_high[z, 12:16]
        k[p, 0:8] = y_low[z, 16:24]
        k[p, 8:24] = k_own[z]
        k[p, 24:32] = y_high[z, 16:24]
    for src, start, k_start in ((z_low, 1, 0), (z_high, 21, 21)):
        for q in range(4):
            for a in range(4):
                part = src[24 * (4 * a + q) : 24 * (4 * a + q) + 24]
                if a < 3:
                    b[a, start + q, 4:28] = part
                else:
                    m[start + q, 4:28] = part
        for q in range(5):
            k[k_start + q] = src[384 + 32 * q : 416 + 32 * q]
    fill_coefficients(k, co, (1, 25), 1.0, 1, m)
    first_sweep((1, 25), b, first, w)
    sweep((2, 24), b, first, u, k, co, 1)

    for z1 in range(-1, 9):
        p = 2 * z1 + 5
        k1[z1 + 1] = block_mean(k[p], k[p + 1], tmp, 1)
    lane = lanes_of(16)
    odd = (lane & 1) != 0
    for z1 in range(8):
        p = 2 * z1 + 5
        rests = [left_over(q, b, u, k, co, 1)[1] for q in (p, p + 1)]
        parts = [
            block_mean(m[p] * rests[0][c], m[p + 1] * rests[1][c], tmp, 1) for c in range(3)
        ]
        centre = k1[z1 + 1]
        sides = jnp.where(lane < 126, lane_next(centre, 2), 0.0) + jnp.where(lane >= 2, lane_prev(centre, 2), 0.0)
        total = 0.125 * (6.0 * centre + sides + row_next(centre) + row_prev(centre) + k1[z1] + k1[z1 + 2])
        message[0, z1] = jnp.where(odd, parts[1], parts[0])[4:12]
        message[1, z1] = jnp.where(odd, centre, parts[2])[4:12]
        message[2, z1] = total[4:12]


def middle_kernel(place, z_low, z_mid, z_high,
                  b1, u1, k1, t1, b2, k2, packed,
                  cx, cy, cz, e, w, first, rest2, cx2, cy2, cz2, e2, w2, u2a, u2b, tmp):
    co = (cx, cy, cz, e, w)
    lane = lanes_of(24)
    odd = (lane & 1) != 0
    for src, start in ((z_low, 0), (z_mid, 8), (z_high, 16)):
        for q in range(8):
            p = start + q
            v = src[0, q]
            b1[0, p] = jnp.where(odd, lane_prev(v, 1), v)
            b1[1, p] = jnp.where(odd, v, lane_next(v, 1))
            v = src[1, q]
            b1[2, p] = jnp.where(odd, lane_prev(v, 1), v)
            k1[p] = jnp.where(odd, v, lane_next(v, 1))
            t1[p] = src[2, q]

    k_top = 23

    def fill(p, carry):
        k_hi = k1[jnp.minimum(p + 1, k_top)]
        cxv, cyv, czv, ev, wv = coefficients(k1[p], k1[p], k_hi, 0.25, 2, None, t1[p])
        cx[p] = cxv
        cy[p] = cyv
        cz[p] = czv
        e[p] = ev
        w[p] = wv
        return carry

    lax.fori_loop(0, 24, fill, 0)
    first_sweep((0, 24), b1, first, w)
    sweep((1, 23), b1, first, u1, k1, co, 2)
    for q2 in range(12):
        k2[q2, 4:16] = block_mean(k1[2 * q2], k1[2 * q2 + 1], tmp, 2)
        k2[q2, 0:4] = jnp.zeros((4, 128), F32)
    for q2 in range(1, 11):
        rests = [left_over(p, b1, u1, k1, co, 2)[1] for p in (2 * q2, 2 * q2 + 1)]
        for c in range(3):
            b2[c, q2, 4:16] = block_mean(rests[0][c], rests[1][c], tmp, 2)
            b2[c, q2, 0:4] = jnp.zeros((4, 128), F32)
    co2 = (cx2, cy2, cz2, e2, w2)
    fill_coefficients(k2, co2, (1, 11), 0.0625, 4)
    first_sweep((1, 11), b2, u2a, w2)
    sweep((2, 10), b2, u2a, u2b, k2, co2, 4)
    j = place[0] // 2
    lane = lanes_of(8)
    group = lane & 7
    pack = jnp.zeros((8, 128), F32)
    for zz in range(2):
        rests = [left_over(p, b2, u2b, k2, co2, 4)[1] for p in (4 + 2 * zz, 5 + 2 * zz)]
        parts = [block_mean(rests[0][c], rests[1][c], tmp, 4) for c in range(3)]
        parts.append(block_mean(k2[4 + 2 * zz], k2[5 + 2 * zz], tmp, 4))
        for a in range(4):
            pack = jnp.where(group == ((j + 2 * a + zz) & 7), parts[a], pack)
    packed[0:2] = pack[4:6]
    quad = lane & 3
    for c in range(3):
        v = u2b[c, 7, 8:16]
        for zz in (2, 1, 0):
            v = jnp.where(quad == zz, u2b[c, 4 + zz, 8:16], v)
        packed[2 + 4 * c : 6 + 4 * c] = v[0:4]
    packed[14:16] = jnp.zeros((2, 128), F32)


def window_kernel(place, received, out, tmp):
    c = place[1]
    for q in range(12):
        peer = c - 6 + q
        inside = jnp.logical_and(peer >= 0, peer < COL).astype(F32)
        tmp[2 * q : 2 * q + 2] = inside * received[jnp.clip(peer, 0, COL - 1), 0:2]
    for q in range(3):
        peer = c - 1 + q
        inside = jnp.logical_and(peer >= 0, peer < COL).astype(F32)
        for comp in range(3):
            part = received[jnp.clip(peer, 0, COL - 1), 2 + 4 * comp : 6 + 4 * comp]
            base = 24 + 12 * comp + 4 * q
            tmp[base : base + 4] = inside * part
    tmp[60:64] = jnp.zeros((4, 128), F32)
    whole = tmp[...]
    for d in range(SLAB):
        out[d] = whole


def upper_kernel(place, received, b2, k2, b1, u1, k1, t1, b0, u0, k0, m0,
                 field, residual,
                 b3, k3, co3, u3a, u3b, co2, u2a, u2b, co1, u1a, u1b, co0, u0a, u0b, tmp):
    d = place[0]
    lane = lanes_of(24)
    group = lane & 7
    for a in range(2):
        for r in range(8):
            mix = jnp.zeros((24, 128), F32)
            for j in range(8):
                mix = jnp.where(group == ((j + r) & 7), received[2 * j + a, 0:24], mix)
            if r:
                mix = jnp.where(group < 8 - r, lane_next(mix, r), lane_prev(mix, 8 - r))
            arr, plane = r // 2, 2 * a + r % 2
            if arr < 3:
                b3[arr, plane] = mix
            else:
                k3[plane] = mix

    def above(v_of, i):
        return v_of(i + 1) if i < 3 else jnp.where(group < 7, lane_next(v_of(0), 1), 0.0)

    def below(v_of, i):
        return v_of(i - 1) if i > 0 else jnp.where(group > 0, lane_prev(v_of(3), 1), 0.0)

    cx3, cy3, cz3, e3, w3 = (co3.at[n] for n in range(5))
    for i in range(4):
        cx, cy, cz, e, w = coefficients(
            k3[i], below(lambda q: k3[q], i), above(lambda q: k3[q], i), 1.0 / 64.0, 8, None
        )
        cx3[i] = cx
        cy3[i] = cy
        cz3[i] = cz
        e3[i] = e
        w3[i] = w
        for c in range(3):
            u3a[c, i] = w * b3[c, i]

    def coarse(src, dst):
        for i in range(4):
            u = [src[c, i] for c in range(3)]
            lo = [below(lambda q: src[c, q], i) for c in range(3)]
            hi = [above(lambda q: src[c, q], i) for c in range(3)]
            b = [b3[c, i] for c in range(3)]
            cz_lo = below(lambda q: cz3[q], i)
            rest = remainder(b, u, lo, hi, k3[i], cx3[i], cy3[i], cz3[i], cz_lo, e3[i], 8)
            for c in range(3):
                dst[c, i] = u[c] + w3[i] * rest[c]

    def two(t, carry):
        coarse(u3a, u3b)
        coarse(u3b, u3a)
        return carry

    lax.fori_loop(0, 3, two, 0)
    coarse(u3a, u3b)

    c2 = tuple(co2.at[n] for n in range(5))
    fill_coefficients(k2, c2, (1, 11), 0.0625, 4)
    c2[2][0] = (0.5 * 0.0625) * (k2[0] + k2[1])
    lane8 = lanes_of(8)
    lane12 = lanes_of(12)
    for q2 in range(12):
        zz = q2 % 4
        peer = d - 1 + q2 // 4
        inside = jnp.logical_and(peer >= 0, peer < SLAB)
        peer = jnp.clip(peer, 0, SLAB - 1)
        pick = jnp.logical_and((lane12 & 3) == zz, inside)
        for c in range(3):
            v = jnp.where(pick, received[peer, 24 + 12 * c : 36 + 12 * c], 0.0)
            u2a[c, q2, 4:16] = spread(v, lane12, 4)
            u2a[c, q2, 0:4] = jnp.zeros((4, 128), F32)
    for t in range(6):
        z = 2 * d - 2 + t
        i = (z + 32) & 3
        j = z >> 2
        for c in range(3):
            v = jnp.where((lane8 & 7) == j, u3b[c, i, 8:16], 0.0)
            double_rows(spread(v, lane8, 8), tmp)
            for q2 in (2 * t, 2 * t + 1):
                u2a[c, q2] = u2a[c, q2] + tmp[0:16]
    sweep((1, 11), b2, u2a, u2b, k2, c2, 4)
    sweep((2, 10), b2, u2b, u2a, k2, c2, 4)

    c1 = tuple(co1.at[n] for n in range(5))

    def fill(p, carry):
        for ref, v in zip(c1, coefficients(k1[p], k1[p], k1[p + 1], 0.25, 2, None, t1[p])):
            ref[p] = v
        return carry

    lax.fori_loop(4, 20, fill, 0)
    for q2 in range(2, 10):
        for c in range(3):
            double_rows(u2a[c, q2], tmp)
            more = tmp[8:32]
            for p in (2 * q2, 2 * q2 + 1):
                u1a[c, p] = u1[c, p] + more
    sweep((5, 19), b1, u1a, u1b, k1, c1, 2)
    sweep((6, 18), b1, u1b, u1a, k1, c1, 2)

    c0 = tuple(co0.at[n] for n in range(5))
    fill_coefficients(k0, c0, (2, 24), 1.0, 1, m0)
    for p1 in range(6, 18):
        for c in range(3):
            double_rows(u1a[c, p1], tmp)
            more = tmp[8:40]
            for p in (2 * p1 - 11, 2 * p1 - 10):
                if 2 <= p < 24:
                    u0a[c, p] = u0[c, p] + m0[p] * more
    sweep((3, 23), b0, u0a, u0b, k0, c0, 1)
    sweep((4, 22), b0, u0b, u0a, k0, c0, 1)

    def last(z, carry):
        p = z + 5
        u, rest = left_over(p, b0, u0a, k0, c0, 1)
        for c in range(3):
            field[c, z] = u[c][8:24]
            residual[c, z] = (m0[p] * rest[c])[8:24]
        return carry

    lax.fori_loop(0, 16, last, 0)


def struct(*shape):
    return jax.ShapeDtypeStruct(shape, F32)


def call(kernel, name, outs, scratch, *args, smem=0):
    vmem = pl.BlockSpec(memory_space=pltpu.VMEM)
    return pl.pallas_call(
        kernel,
        name=name,
        out_shape=outs,
        in_specs=[pl.BlockSpec(memory_space=pltpu.SMEM)] * smem + [vmem] * (len(args) - smem),
        out_specs=jax.tree.map(lambda _: vmem, outs),
        scratch_shapes=[pltpu.VMEM(s, F32) for s in scratch],
        compiler_params=pltpu.CompilerParams(vmem_limit_bytes=40 * 1024 * 1024),
    )(*args)


def shift(block, axis, count, by):
    pairs = [(i, i + by) for i in range(count) if 0 <= i + by < count]
    return lax.ppermute(block, axis, pairs)


def on_device(load, density, moduli, fixed):
    place = jnp.stack([lax.axis_index("slab"), lax.axis_index("col")]).astype(jnp.int32)
    k, m, low, high = call(
        prep_kernel, "prep",
        (struct(16, 16, 128), struct(16, 16, 128), struct(16, 24, 128), struct(16, 24, 128)),
        [], moduli, load, density, fixed, smem=1,
    )
    y_low = shift(high, "col", COL, 1)
    y_high = shift(low, "col", COL, -1)
    low, high = call(
        planes_kernel, "planes", (struct(544, 128), struct(544, 128)), [], load, k, m, y_low, y_high
    )
    z_low = shift(high, "slab", SLAB, 1)
    z_high = shift(low, "slab", SLAB, -1)
    full0, full0v = (26, 32, 128), (3, 26, 32, 128)
    b0, u0, k0, m0, message = call(
        fine_kernel, "fine",
        (struct(*full0v), struct(*full0v), struct(*full0), struct(*full0), struct(3, 8, 8, 128)),
        [full0] * 5 + [full0v, (10, 16, 128), (32, 128)],
        load, k, m, y_low, y_high, z_low, z_high,
    )
    y_low = shift(message, "col", COL, 1)
    y_high = shift(message, "col", COL, -1)
    wide = jnp.concatenate([y_low, message, y_high], axis=2)
    z_low = shift(wide, "slab", SLAB, 1)
    z_high = shift(wide, "slab", SLAB, -1)
    full1, full1v = (24, 24, 128), (3, 24, 24, 128)
    full2, full2v = (12, 16, 128), (3, 12, 16, 128)
    b1, u1, k1, t1, b2, k2, packed = call(
        middle_kernel, "middle",
        (struct(*full1v), struct(*full1v), struct(*full1), struct(*full1), struct(*full2v), struct(*full2),
         struct(16, 128)),
        [full1] * 5 + [full1v, full1v] + [full2] * 5 + [full2v, full2v, (32, 128)],
        place, z_low, wide, z_high, smem=1,
    )
    received = lax.all_to_all(jnp.broadcast_to(packed, (COL, 16, 128)), "col", 0, 0)
    window = call(window_kernel, "window", struct(SLAB, 64, 128), [(64, 128)], place, received, smem=1)
    received = lax.all_to_all(window, "slab", 0, 0)
    full3, full3v = (4, 24, 128), (3, 4, 24, 128)
    return call(
        upper_kernel, "upper",
        (struct(3, 16, 16, 128), struct(3, 16, 16, 128)),
        [full3v, full3, (5,) + full3, full3v, full3v, (5,) + full2, full2v, full2v,
         (5,) + full1, full1v, full1v, (5,) + full0, full0v, full0v, (48, 128)],
        place, received, b2, k2, b1, u1, k1, t1, b0, u0, k0, m0, smem=1,
    )


def solution(mesh):
    placed = (P(None, "slab", "col", None), P("slab", "col", None), P(), P("slab", "col", None))
    return jax.shard_map(
        on_device,
        mesh=mesh,
        in_specs=placed,
        out_specs=(P(None, "slab", "col", None), P(None, "slab", "col", None)),
        check_vma=False,
    )
```

```python
import jax
import jax.numpy as jnp
from jax import lax
from jax.experimental import pallas as pl
from jax.experimental.pallas import tpu as pltpu
from jax.sharding import PartitionSpec as P

CLASSES = 8
OMEGA = 0.6
COUPLE = 0.05
SLAB = 16
COL = 32
F32 = jnp.float32

UNROLL = 8


def each(planes, body, unroll=None):
    unroll = unroll or UNROLL
    low, high = planes
    rounds = (high - low) // unroll
    if rounds > 1:
        def chunk(t, carry):
            for q in range(unroll):
                body(low + t * unroll + q)
            return carry

        lax.fori_loop(0, rounds, chunk, 0)
        low += rounds * unroll
    for p in range(low, high):
        body(p)


def lanes_of(rows):
    return lax.broadcasted_iota(jnp.int32, (rows, 128), 1)


def lane_next(v, step):
    return pltpu.roll(v, 128 - step, 1)


def lane_prev(v, step):
    return pltpu.roll(v, step, 1)


def row_next(v):
    return pltpu.roll(v, v.shape[0] - 1, 0)


def row_prev(v):
    return pltpu.roll(v, 1, 0)


def spread(v, lane, width):
    step = 1
    while step < width:
        v = v + jnp.where((lane & step) != 0, lane_prev(v, step), lane_next(v, step))
        step *= 2
    return v


def coefficients(k, k_lo, k_hi, scale, step, mask, total=None):
    lane = lanes_of(k.shape[0])
    half = 0.5 * scale
    k_next = lane_next(k, step)
    cx = jnp.where(lane < 128 - step, half * (k + k_next), 0.0)
    ky = row_next(k)
    cy = half * (k + ky)
    cz = half * (k + k_hi)
    if total is None:
        sides = jnp.where(lane < 128 - step, k_next, 0.0) + jnp.where(lane >= step, lane_prev(k, step), 0.0)
        total = half * (6.0 * k + sides + ky + row_prev(k) + k_lo + k_hi)
    diag = total + 2.0 * COUPLE * k
    top = OMEGA if mask is None else OMEGA * mask
    weight = jnp.where(k > 0.0, top / diag, 0.0)
    return cx, cy, cz, total + COUPLE * k, weight


def remainder(b, u, u_lo, u_hi, k, cx, cy, cz, cz_lo, e, step):
    cx_lo = lane_prev(cx, step)
    cy_lo = row_prev(cy)
    shared = COUPLE * k * (u[0] + u[1] + u[2])
    out = []
    for c in range(3):
        v = u[c]
        around = cx * lane_next(v, step) + cx_lo * lane_prev(v, step)
        around = around + cy * row_next(v) + cy_lo * row_prev(v)
        around = around + cz * u_hi[c] + cz_lo * u_lo[c]
        out.append((b[c] - shared) + (around - e * v))
    return out


def fill_coefficients(k_ref, co, planes, scale, step, total_ref=None):
    def body(p):
        total = None if total_ref is None else total_ref[p]
        values = coefficients(k_ref[p], k_ref[p - 1], k_ref[p + 1], scale, step, None, total)
        for ref, v in zip(co, values):
            ref[p] = v

    each(planes, body)


def fine_coefficients(k_ref, m_ref, co, planes):
    def body(p):
        k = k_ref[p, 4:28]
        k_lo, k_hi = k_ref[p - 1, 4:28], k_ref[p + 1, 4:28]
        ky, ky_lo = k_ref[p, 5:29], k_ref[p, 3:27]
        lane = lanes_of(24)
        k_next = jnp.where(lane < 127, lane_next(k, 1), 0.0)
        k_prev = jnp.where(lane >= 1, lane_prev(k, 1), 0.0)
        total = 0.5 * (6.0 * k + k_next + k_prev + ky + ky_lo + k_lo + k_hi)
        values = (
            jnp.where(lane < 127, 0.5 * (k + k_next), 0.0), 0.5 * (k + ky), 0.5 * (k + k_hi),
            total + COUPLE * k,
            jnp.where(k > 0.0, OMEGA * m_ref[p] / (total + 2.0 * COUPLE * k), 0.0),
        )
        for ref, v in zip(co, values):
            ref[p] = v

    each(planes, body)


def left_over(p, b_ref, u_ref, k_ref, co, step, rows=slice(None)):
    cx_ref, cy_ref, cz_ref, e_ref, _ = co
    b = [b_ref[c, p] for c in range(3)]
    u = [u_ref[c, p] for c in range(3)]
    lo = [u_ref[c, p - 1] for c in range(3)]
    hi = [u_ref[c, p + 1] for c in range(3)]
    k = k_ref[p, rows]
    return u, remainder(b, u, lo, hi, k, cx_ref[p], cy_ref[p], cz_ref[p], cz_ref[p - 1], e_ref[p], step)


def sweep(planes, b_ref, u_ref, new_ref, k_ref, co, step, rows=slice(None)):
    def body(p):
        u, rest = left_over(p, b_ref, u_ref, k_ref, co, step, rows)
        w = co[4][p]
        for c in range(3):
            new_ref[c, p] = u[c] + w * rest[c]

    each(planes, body)


def first_sweep(planes, b_ref, new_ref, w_ref):
    def body(p):
        w = w_ref[p]
        for c in range(3):
            new_ref[c, p] = w * b_ref[c, p]

    each(planes, body)


def block_mean(a, b, tmp, step):
    lane = lanes_of(a.shape[0])
    s = a + b
    s = s + jnp.where((lane & step) != 0, lane_prev(s, step), lane_next(s, step))
    n = a.shape[0]
    tmp[0:n] = s
    return 0.125 * (tmp[pl.ds(0, n // 2, stride=2)] + tmp[pl.ds(1, n // 2, stride=2)])


def double_rows(v, tmp):
    n = v.shape[0]
    tmp[pl.ds(0, n, stride=2)] = v
    tmp[pl.ds(1, n, stride=2)] = v


FINE = slice(4, 28)


def prep_kernel(moduli_in, load_in, density_in, fixed_in, load, k_out, m_out, low, high, moduli, density, fixed, sems):
    copies = [
        pltpu.make_async_copy(src, dst, sems.at[n])
        for n, (src, dst) in enumerate(
            ((moduli_in, moduli), (density_in, density), (fixed_in, fixed), (load_in, load))
        )
    ]
    for copy in copies:
        copy.start()
    for copy in copies[:3]:
        copy.wait()
    for z in range(16):
        d = density[z]
        k = jnp.zeros((16, 128), F32)
        for klass in range(CLASSES):
            k = jnp.where(d == klass, moduli[klass], k)
        m = 1.0 - fixed[z].astype(F32)
        k_out[z] = k
        m_out[z] = m
        low[z, 12:16] = m[0:4]
        high[z, 12:16] = m[12:16]
        low[z, 16:24] = k[0:8]
        high[z, 16:24] = k[8:16]
    copies[3].wait()
    for z in range(16):
        for c in range(3):
            low[z, 4 * c : 4 * c + 4] = load[c, z, 0:4]
            high[z, 4 * c : 4 * c + 4] = load[c, z, 12:16]


def planes_kernel(place, load, k, m, from_low, from_high, partner, cross):
    odd = place[0] & 1
    for out, start, k_start in (
        (partner, 12 * (1 - odd), 11 * (1 - odd)), (cross, 12 * odd, 11 * odd),
    ):
        for q in range(4):
            z = start + q
            for a in range(4):
                base = 24 * (4 * a + q)
                own = load[a, z] if a < 3 else m[z]
                out[base : base + 4] = from_low[z, 4 * a : 4 * a + 4]
                out[base + 4 : base + 20] = own
                out[base + 20 : base + 24] = from_high[z, 4 * a : 4 * a + 4]
        for q in range(5):
            z = k_start + q
            base = 384 + 32 * q
            out[base : base + 8] = from_low[z, 16:24]
            out[base + 8 : base + 24] = k[z]
            out[base + 24 : base + 32] = from_high[z, 16:24]


def fine_kernel(place, load, k_own, m_own, y_low, y_high, partner, cross,
                b, u, k, m, message,
                cx, cy, cz, e, w, first, k1, tmp):
    co = (cx, cy, cz, e, w)
    odd = place[0] & 1
    for z in range(16):
        p = z + 5
        for c in range(3):
            b[c, p, 0:4] = y_low[z, 4 * c : 4 * c + 4]
            b[c, p, 4:20] = load[c, z]
            b[c, p, 20:24] = y_high[z, 4 * c : 4 * c + 4]
        m[p, 0:4] = y_low[z, 12:16]
        m[p, 4:20] = m_own[z]
        m[p, 20:24] = y_high[z, 12:16]
        k[p, 0:8] = y_low[z, 16:24]
        k[p, 8:24] = k_own[z]
        k[p, 24:32] = y_high[z, 16:24]
    for src, high in ((partner.at[1 - odd], 1 - odd), (cross, odd)):
        start, k_start = 1 + 20 * high, 21 * high
        for q in range(4):
            for a in range(4):
                part = src[24 * (4 * a + q) : 24 * (4 * a + q) + 24]
                if a < 3:
                    b[a, start + q] = part
                else:
                    m[start + q] = part
        for q in range(5):
            k[k_start + q] = src[384 + 32 * q : 416 + 32 * q]
    fine_coefficients(k, m, co, (1, 25))
    first_sweep((1, 25), b, first, w)
    sweep((2, 24), b, first, u, k, co, 1, FINE)

    for z1 in range(-1, 9):
        p = 2 * z1 + 5
        k1[z1 + 1] = block_mean(k[p], k[p + 1], tmp.at[(z1 + 1) % 4], 1)
    lane = lanes_of(8)
    odd_lane = (lane & 1) != 0
    lane = lanes_of(16)
    for z1 in range(8):
        p = 2 * z1 + 5
        rests = [left_over(q, b, u, k, co, 1, FINE)[1] for q in (p, p + 1)]
        parts = [
            block_mean(m[p] * rests[0][c], m[p + 1] * rests[1][c], tmp.at[c], 1)[2:10] for c in range(3)
        ]
        centre = k1[z1 + 1]
        sides = jnp.where(lane < 126, lane_next(centre, 2), 0.0) + jnp.where(lane >= 2, lane_prev(centre, 2), 0.0)
        total = 0.125 * (6.0 * centre + sides + row_next(centre) + row_prev(centre) + k1[z1] + k1[z1 + 2])
        message[0, z1] = jnp.where(odd_lane, parts[1], parts[0])
        message[1, z1] = jnp.where(odd_lane, centre[4:12], parts[2])
        message[2, z1] = total[4:12]


def middle_kernel(place, own, partner, cross,
                  b1_out, u1_out, k1_out, t1_out, b2, k2, u2b, packed,
                  b1, u1, k1, t1, cx, cy, cz, e, w, first, cx2, cy2, cz2, e2, w2, u2a, tmp):
    co = (cx, cy, cz, e, w)
    lane = lanes_of(24)
    odd_lane = (lane & 1) != 0
    odd = place[0] & 1
    for src, start in ((own, 8), (partner.at[1 - odd], 16 * (1 - odd)), (cross, 16 * odd)):
        for q in range(8):
            p = start + q
            v = src[0, q]
            b1[0, p] = jnp.where(odd_lane, lane_prev(v, 1), v)
            b1[1, p] = jnp.where(odd_lane, v, lane_next(v, 1))
            v = src[1, q]
            b1[2, p] = jnp.where(odd_lane, lane_prev(v, 1), v)
            k1[p] = jnp.where(odd_lane, v, lane_next(v, 1))
            t1[p] = src[2, q]
    k1[24] = jnp.zeros((24, 128), F32)

    def fill(p):
        for ref, v in zip(co, coefficients(k1[p], None, k1[p + 1], 0.25, 2, None, t1[p])):
            ref[p] = v
        for c in range(3):
            first[c, p] = w[p] * b1[c, p]

    each((0, 24), fill)
    sweep((1, 23), b1, first, u1, k1, co, 2)
    for p in range(16):
        k1_out[p] = k1[p + 4, 4:20]
        t1_out[p] = t1[p + 4, 4:20]
        for c in range(3):
            b1_out[c, p] = b1[c, p + 4, 4:20]
            u1_out[c, p] = u1[c, p + 4, 4:20]
    for q2 in range(12):
        k2[q2, 4:16] = block_mean(k1[2 * q2], k1[2 * q2 + 1], tmp.at[q2 % 4], 2)
        k2[q2, 0:4] = jnp.zeros((4, 128), F32)
    for q2 in range(1, 11):
        rests = [left_over(p, b1, u1, k1, co, 2)[1] for p in (2 * q2, 2 * q2 + 1)]
        for c in range(3):
            b2[c, q2, 4:16] = block_mean(rests[0][c], rests[1][c], tmp.at[c], 2)
            b2[c, q2, 0:4] = jnp.zeros((4, 128), F32)
    co2 = (cx2, cy2, cz2, e2, w2)
    fill_coefficients(k2, co2, (1, 11), 0.0625, 4)
    first_sweep((1, 11), b2, u2a, w2)
    sweep((2, 10), b2, u2a, u2b, k2, co2, 4)
    j = place[0] // 2
    lane = lanes_of(8)
    group = lane & 7
    pack = jnp.zeros((8, 128), F32)
    for zz in range(2):
        rests = [left_over(p, b2, u2b, k2, co2, 4)[1] for p in (4 + 2 * zz, 5 + 2 * zz)]
        parts = [block_mean(rests[0][c], rests[1][c], tmp.at[c], 4) for c in range(3)]
        parts.append(block_mean(k2[4 + 2 * zz], k2[5 + 2 * zz], tmp.at[3], 4))
        for a in range(4):
            pack = jnp.where(group == ((j + 2 * a + zz) & 7), parts[a], pack)
    quad = lane & 3
    low, high = tmp.at[0], tmp.at[1]
    low[0:2] = pack[4:6]
    high[0:2] = pack[4:6]
    for c in range(3):
        v = u2b[c, 7, 8:16]
        for zz in (2, 1, 0):
            v = jnp.where(quad == zz, u2b[c, 4 + zz, 8:16], v)
        low[2 + 2 * c : 4 + 2 * c] = v[2:4]
        high[2 + 2 * c : 4 + 2 * c] = v[0:2]
    to_low, to_high = low[0:8], high[0:8]
    for peer in range(COL):
        packed[peer] = jnp.where(place[1] < peer, to_high, to_low)


def window_kernel(place, received, u2, out, tmp):
    c, d = place[1], place[0]
    for q in range(11):
        peer = c - 5 + q
        inside = jnp.logical_and(peer >= 0, peer < COL).astype(F32)
        tmp[2 * q : 2 * q + 2] = inside * received[jnp.clip(peer, 0, COL - 1), 0:2]
    for comp in range(3):
        for q, peer in ((0, c - 1), (1, c + 1)):
            inside = jnp.logical_and(peer >= 0, peer < COL).astype(F32)
            part = received[jnp.clip(peer, 0, COL - 1), 2 + 2 * comp : 4 + 2 * comp]
            base = 22 + 4 * comp + 2 * q
            tmp[base : base + 2] = inside * part
    quad = lanes_of(4) & 3
    tmp[46:48] = jnp.zeros((2, 128), F32)

    def inner(near):
        for comp in range(3):
            a = [u2[comp, 4 + near + f, 6:10] for f in range(2)]
            b = [u2[comp, 4 + near + f, 10:14] for f in range(2)]
            v = jnp.where(quad == 0, a[0], jnp.where(quad == 1, a[1], jnp.where(quad == 2, b[0], b[1])))
            tmp[34 + 4 * comp : 38 + 4 * comp] = v
        return tmp[...]

    to_high = inner(0)
    to_low = inner(2)
    for peer in range(SLAB):
        out[peer] = jnp.where(d < peer, to_high, to_low)


def upper_kernel(place, received, u2, b2, k2, b1, u1, k1, t1, b0, u0, k0, m0,
                 field, residual,
                 b3, k3, co3, u3a, u3b, co2, u2a, u2b, co1, u1a, u1b, co0, u0a, u0b, tmp):
    d = place[0]
    lane = lanes_of(24)
    group = lane & 7
    for a in range(2):
        for r in range(8):
            mix = jnp.zeros((24, 128), F32)
            for j in range(8):
                mix = jnp.where(group == ((j + r) & 7), received[2 * j + a, 0:24], mix)
            if r:
                mix = jnp.where(group < 8 - r, lane_next(mix, r), lane_prev(mix, 8 - r))
            arr, plane = r // 2, 2 * a + r % 2
            if arr < 3:
                b3[arr, plane] = mix
            else:
                k3[plane] = mix

    def above(v_of, i):
        return v_of(i + 1) if i < 3 else jnp.where(group < 7, lane_next(v_of(0), 1), 0.0)

    def below(v_of, i):
        return v_of(i - 1) if i > 0 else jnp.where(group > 0, lane_prev(v_of(3), 1), 0.0)

    cx3, cy3, cz3, e3, w3 = (co3.at[n] for n in range(5))
    for i in range(4):
        cx, cy, cz, e, w = coefficients(
            k3[i], below(lambda q: k3[q], i), above(lambda q: k3[q], i), 1.0 / 64.0, 8, None
        )
        cx3[i] = cx
        cy3[i] = cy
        cz3[i] = cz
        e3[i] = e
        w3[i] = w
        for c in range(3):
            u3a[c, i] = w * b3[c, i]

    def coarse(src, dst):
        for i in range(4):
            u = [src[c, i] for c in range(3)]
            lo = [below(lambda q: src[c, q], i) for c in range(3)]
            hi = [above(lambda q: src[c, q], i) for c in range(3)]
            b = [b3[c, i] for c in range(3)]
            cz_lo = below(lambda q: cz3[q], i)
            rest = remainder(b, u, lo, hi, k3[i], cx3[i], cy3[i], cz3[i], cz_lo, e3[i], 8)
            for c in range(3):
                dst[c, i] = u[c] + w3[i] * rest[c]

    def two(t, carry):
        coarse(u3a, u3b)
        coarse(u3b, u3a)
        return carry

    lax.fori_loop(0, 3, two, 0)
    coarse(u3a, u3b)

    c2 = tuple(co2.at[n] for n in range(5))
    fill_coefficients(k2, c2, (1, 11), 0.0625, 4)
    c2[2][0] = (0.5 * 0.0625) * (k2[0] + k2[1])
    lane8 = lanes_of(8)
    lane4 = lanes_of(4)
    for q2 in range(12):
        zz = q2 % 4
        peer = d - 1 + q2 // 4
        inside = jnp.logical_and(peer >= 0, peer < SLAB)
        peer = jnp.clip(peer, 0, SLAB - 1)
        far = q2 if q2 < 2 else q2 - 10 if q2 >= 10 else None
        for c in range(3):
            v = jnp.where(jnp.logical_and((lane4 & 3) == zz, inside), received[peer, 22 + 4 * c : 26 + 4 * c], 0.0)
            v = spread(v, lane4, 4)
            u2a[c, q2, 0:4] = jnp.zeros((4, 128), F32)
            u2a[c, q2, 4:6] = v[0:2]
            u2a[c, q2, 14:16] = v[2:4]
            if far is None:
                u2a[c, q2, 6:14] = u2[c, q2, 6:14]
            else:
                v = received[peer, 34 + 4 * c : 38 + 4 * c]
                for half in range(2):
                    pick = jnp.logical_and((lane4 & 3) == 2 * half + far, inside)
                    u2a[c, q2, 6 + 4 * half : 10 + 4 * half] = spread(jnp.where(pick, v, 0.0), lane4, 4)
    for t in range(6):
        z = 2 * d - 2 + t
        i = (z + 32) & 3
        j = z >> 2
        for c in range(3):
            v = jnp.where((lane8 & 7) == j, u3b[c, i, 8:16], 0.0)
            double_rows(spread(v, lane8, 8), tmp.at[c])
            for q2 in (2 * t, 2 * t + 1):
                u2a[c, q2, 4:16] = u2a[c, q2, 4:16] + tmp[c, 0:12]
    sweep((1, 11), b2, u2a, u2b, k2, c2, 4)
    sweep((2, 10), b2, u2b, u2a, k2, c2, 4)

    c1 = tuple(co1.at[n] for n in range(5))

    def fill(p):
        for ref, v in zip(c1, coefficients(k1[p], None, k1[p + 1], 0.25, 2, None, t1[p])):
            ref[p] = v

    each((0, 15), fill)
    for q2 in range(2, 10):
        for c in range(3):
            double_rows(u2a[c, q2, 6:14], tmp.at[c])
            more = tmp[c, 0:16]
            for p in (2 * q2 - 4, 2 * q2 - 3):
                u1a[c, p] = u1[c, p] + more
    sweep((1, 15), b1, u1a, u1b, k1, c1, 2)
    sweep((2, 14), b1, u1b, u1a, k1, c1, 2)

    c0 = tuple(co0.at[n] for n in range(5))
    fine_coefficients(k0, m0, c0, (2, 24))
    for p1 in range(2, 14):
        for c in range(3):
            double_rows(u1a[c, p1], tmp.at[c])
            more = tmp[c, 4:28]
            for p in (2 * p1 - 3, 2 * p1 - 2):
                if 2 <= p < 24:
                    u0a[c, p] = u0[c, p] + m0[p] * more
    sweep((3, 23), b0, u0a, u0b, k0, c0, 1, FINE)
    sweep((4, 22), b0, u0b, u0a, k0, c0, 1, FINE)

    def last(z):
        p = z + 5
        u, rest = left_over(p, b0, u0a, k0, c0, 1, FINE)
        for c in range(3):
            field[c, z] = u[c][4:20]
            residual[c, z] = (m0[p] * rest[c])[4:20]

    each((0, 16), last)


def struct(*shape):
    return jax.ShapeDtypeStruct(shape, F32)


def call(kernel, name, outs, scratch, *args, smem=0, hbm=0):
    vmem = pl.BlockSpec(memory_space=pltpu.VMEM)
    specs = [pl.BlockSpec(memory_space=pltpu.SMEM)] * smem + [pl.BlockSpec(memory_space=pltpu.HBM)] * hbm
    return pl.pallas_call(
        kernel,
        name=name,
        out_shape=outs,
        in_specs=specs + [vmem] * (len(args) - len(specs)),
        out_specs=jax.tree.map(lambda _: vmem, outs),
        scratch_shapes=[pltpu.VMEM(s, F32) if isinstance(s, tuple) else s for s in scratch],
        compiler_params=pltpu.CompilerParams(vmem_limit_bytes=40 * 1024 * 1024),
    )(*args)


def shift(block, axis, count, by):
    pairs = [(i, i + by) for i in range(count) if 0 <= i + by < count]
    return lax.ppermute(block, axis, pairs)


def slab_neighbours(to_partner, to_cross):
    pairs = []
    for i in range(1, SLAB - 1, 2):
        pairs += [(i, i + 1), (i + 1, i)]
    cross = lax.ppermute(to_cross, "slab", pairs)
    groups = [[i, i + 1] for i in range(0, SLAB, 2)]
    return lax.all_gather(to_partner, "slab", axis_index_groups=groups), cross


def on_device(load, density, moduli, fixed):
    place = jnp.stack([lax.axis_index("slab"), lax.axis_index("col")]).astype(jnp.int32)
    own = struct(16, 16, 128)
    whole_int = pltpu.VMEM((16, 16, 128), jnp.int32)
    load, k, m, low, high = call(
        prep_kernel, "prep",
        (struct(3, 16, 16, 128), own, own, struct(16, 24, 128), struct(16, 24, 128)),
        [pltpu.SMEM((8,), F32), whole_int, whole_int, pltpu.SemaphoreType.DMA((4,))], moduli, load, density, fixed, hbm=4,
    )
    y_low = shift(high, "col", COL, 1)
    y_high = shift(low, "col", COL, -1)
    to_partner, to_cross = call(
        planes_kernel, "planes", (struct(544, 128), struct(544, 128)), [],
        place, load, k, m, y_low, y_high, smem=1,
    )
    partner, cross = slab_neighbours(to_partner, to_cross)
    part0, full0, full0v = (26, 24, 128), (26, 32, 128), (3, 26, 24, 128)
    b0, u0, k0, m0, message = call(
        fine_kernel, "fine",
        (struct(*full0v), struct(*full0v), struct(*full0), struct(*part0), struct(3, 8, 8, 128)),
        [part0] * 5 + [full0v, (10, 16, 128), (4, 48, 128)],
        place, load, k, m, y_low, y_high, partner, cross, smem=1,
    )
    y_low = shift(message, "col", COL, 1)
    y_high = shift(message, "col", COL, -1)
    wide = jnp.concatenate([y_low, message, y_high], axis=2)
    partner, cross = slab_neighbours(wide, wide)
    full1, full1v, more1 = (24, 24, 128), (3, 24, 24, 128), (25, 24, 128)
    part1, part1v = (16, 16, 128), (3, 16, 16, 128)
    full2, full2v = (12, 16, 128), (3, 12, 16, 128)
    b1, u1, k1, t1, b2, k2, u2, packed = call(
        middle_kernel, "middle",
        (struct(*part1v), struct(*part1v), struct(*part1), struct(*part1), struct(*full2v), struct(*full2),
         struct(*full2v), struct(COL, 8, 128)),
        [full1v, full1v, more1, full1] + [full1] * 5 + [full1v] + [full2] * 5 + [full2v, (4, 48, 128)],
        place, wide, partner, cross, smem=1,
    )
    received = lax.all_to_all(packed, "col", 0, 0)
    window = call(window_kernel, "window", struct(SLAB, 48, 128), [(48, 128)], place, received, u2, smem=1)
    received = lax.all_to_all(window, "slab", 0, 0)
    full3, full3v = (4, 24, 128), (3, 4, 24, 128)
    return call(
        upper_kernel, "upper",
        (struct(3, 16, 16, 128), struct(3, 16, 16, 128)),
        [full3v, full3, (5,) + full3, full3v, full3v, (5,) + full2, full2v, full2v,
         (5,) + part1, part1v, part1v, (5,) + part0, full0v, full0v, (4, 48, 128)],
        place, received, u2, b2, k2, b1, u1, k1, t1, b0, u0, k0, m0, smem=1,
    )


def solution(mesh):
    placed = (P(None, "slab", "col", None), P("slab", "col", None), P(), P("slab", "col", None))
    return jax.shard_map(
        on_device,
        mesh=mesh,
        in_specs=placed,
        out_specs=(P(None, "slab", "col", None), P(None, "slab", "col", None)),
        check_vma=False,
    )
```

```python
import jax
import jax.numpy as jnp
from jax import lax
from jax.experimental import pallas as pl
from jax.experimental.pallas import tpu as pltpu
from jax.sharding import PartitionSpec as P

CLASSES = 8
OMEGA = 0.6
COUPLE = 0.05
SLAB = 16
COL = 32
F32 = jnp.float32


def loop(low, high, body, unroll):
    def step(t, carry):
        for q in range(unroll):
            body(low + t * unroll + q, q)
        return carry

    assert (high - low) % unroll == 0
    lax.fori_loop(0, (high - low) // unroll, step, 0)


def each(planes, body):
    count = planes[1] - planes[0]
    fits = [n for n in (8, 7, 6, 5, 4, 11, 3) if count % n == 0]
    loop(*planes, lambda p, q: body(p), fits[0])


def lanes_of(rows):
    return lax.broadcasted_iota(jnp.int32, (rows, 128), 1)


def lane_next(v, step):
    return pltpu.roll(v, 128 - step, 1)


def lane_prev(v, step):
    return pltpu.roll(v, step, 1)


def row_next(v):
    return pltpu.roll(v, v.shape[0] - 1, 0)


def row_prev(v):
    return pltpu.roll(v, 1, 0)


def spread(v, lane, width):
    step = 1
    while step < width:
        v = v + jnp.where((lane & step) != 0, lane_prev(v, step), lane_next(v, step))
        step *= 2
    return v


def coefficients(k, k_lo, k_hi, scale, step, mask, total=None):
    lane = lanes_of(k.shape[0])
    half = 0.5 * scale
    k_next = lane_next(k, step)
    cx = jnp.where(lane < 128 - step, half * (k + k_next), 0.0)
    ky = row_next(k)
    cy = half * (k + ky)
    cz = half * (k + k_hi)
    if total is None:
        sides = jnp.where(lane < 128 - step, k_next, 0.0) + jnp.where(lane >= step, lane_prev(k, step), 0.0)
        total = half * (6.0 * k + sides + ky + row_prev(k) + k_lo + k_hi)
    diag = total + 2.0 * COUPLE * k
    top = OMEGA if mask is None else OMEGA * mask
    weight = jnp.where(k > 0.0, top / diag, 0.0)
    return cx, cy, cz, total + COUPLE * k, weight


def remainder(b, u, u_lo, u_hi, k, cx, cy, cz, cz_lo, e, step):
    cx_lo = lane_prev(cx, step)
    cy_lo = row_prev(cy)
    shared = COUPLE * k * (u[0] + u[1] + u[2])
    out = []
    for c in range(3):
        v = u[c]
        around = cx * lane_next(v, step) + cx_lo * lane_prev(v, step)
        around = around + cy * row_next(v) + cy_lo * row_prev(v)
        around = around + cz * u_hi[c] + cz_lo * u_lo[c]
        out.append((b[c] - shared) + (around - e * v))
    return out


def fill_coefficients(k_ref, co, planes, scale, step, total_ref=None):
    def body(p):
        total = None if total_ref is None else total_ref[p]
        values = coefficients(k_ref[p], k_ref[p - 1], k_ref[p + 1], scale, step, None, total)
        for ref, v in zip(co, values):
            ref[p] = v

    each(planes, body)


def fine_coefficients(k_ref, m_ref, co, planes):
    def body(p):
        k = k_ref[p, 4:28]
        k_lo, k_hi = k_ref[p - 1, 4:28], k_ref[p + 1, 4:28]
        ky, ky_lo = k_ref[p, 5:29], k_ref[p, 3:27]
        lane = lanes_of(24)
        k_next = jnp.where(lane < 127, lane_next(k, 1), 0.0)
        k_prev = jnp.where(lane >= 1, lane_prev(k, 1), 0.0)
        total = 0.5 * (6.0 * k + k_next + k_prev + ky + ky_lo + k_lo + k_hi)
        values = (
            jnp.where(lane < 127, 0.5 * (k + k_next), 0.0), 0.5 * (k + ky), 0.5 * (k + k_hi),
            total + COUPLE * k,
            jnp.where(k > 0.0, OMEGA * m_ref[p] / (total + 2.0 * COUPLE * k), 0.0),
        )
        for ref, v in zip(co, values):
            ref[p] = v

    each(planes, body)


def left_over(p, b_ref, u_ref, k_ref, co, step, rows=slice(None)):
    cx_ref, cy_ref, cz_ref, e_ref, _ = co
    b = [b_ref[c, p] for c in range(3)]
    u = [u_ref[c, p] for c in range(3)]
    lo = [u_ref[c, p - 1] for c in range(3)]
    hi = [u_ref[c, p + 1] for c in range(3)]
    k = k_ref[p, rows]
    return u, remainder(b, u, lo, hi, k, cx_ref[p], cy_ref[p], cz_ref[p], cz_ref[p - 1], e_ref[p], step)


def sweep(planes, b_ref, u_ref, new_ref, k_ref, co, step, rows=slice(None)):
    def body(p):
        u, rest = left_over(p, b_ref, u_ref, k_ref, co, step, rows)
        w = co[4][p]
        for c in range(3):
            new_ref[c, p] = u[c] + w * rest[c]

    each(planes, body)


def first_sweep(planes, b_ref, new_ref, w_ref):
    def body(p):
        w = w_ref[p]
        for c in range(3):
            new_ref[c, p] = w * b_ref[c, p]

    each(planes, body)


def block_mean(a, b, tmp, step):
    lane = lanes_of(a.shape[0])
    s = a + b
    s = s + jnp.where((lane & step) != 0, lane_prev(s, step), lane_next(s, step))
    n = a.shape[0]
    tmp[0:n] = s
    return 0.125 * (tmp[pl.ds(0, n // 2, stride=2)] + tmp[pl.ds(1, n // 2, stride=2)])


def double_rows(v, tmp):
    n = v.shape[0]
    tmp[pl.ds(0, n, stride=2)] = v
    tmp[pl.ds(1, n, stride=2)] = v


FINE = slice(4, 28)


def prep_kernel(moduli, raw, k_out, m_out, low, high):
    def body(z):
        d = raw[3, z]
        k = jnp.zeros((16, 128), F32)
        for klass in range(CLASSES):
            k = jnp.where(d == float(klass), moduli[klass], k)
        m = 1.0 - raw[4, z]
        k_out[z] = k
        m_out[z] = m
        for c in range(3):
            low[z, 4 * c : 4 * c + 4] = raw[c, z, 0:4]
            high[z, 4 * c : 4 * c + 4] = raw[c, z, 12:16]
        low[z, 12:16] = m[0:4]
        high[z, 12:16] = m[12:16]
        low[z, 16:24] = k[0:8]
        high[z, 16:24] = k[8:16]

    each((0, 16), body)


def planes_kernel(place, load, k, m, from_low, from_high, partner, cross):
    odd = place[0] & 1
    for out, start, k_start in (
        (partner, 12 * (1 - odd), 11 * (1 - odd)), (cross, 12 * odd, 11 * odd),
    ):
        for q in range(4):
            z = start + q
            for a in range(4):
                base = 24 * (4 * a + q)
                own = load[a, z] if a < 3 else m[z]
                out[base : base + 4] = from_low[z, 4 * a : 4 * a + 4]
                out[base + 4 : base + 20] = own
                out[base + 20 : base + 24] = from_high[z, 4 * a : 4 * a + 4]
        for q in range(5):
            z = k_start + q
            base = 384 + 32 * q
            out[base : base + 8] = from_low[z, 16:24]
            out[base + 8 : base + 24] = k[z]
            out[base + 24 : base + 32] = from_high[z, 16:24]


def fine_kernel(place, load, k_own, m_own, y_low, y_high, partner, cross,
                b, u, k, m, message,
                co_out, first, k1, sums, tmp):
    co = tuple(co_out.at[n] for n in range(5))
    w = co[4]
    odd = place[0] & 1
    for z in range(16):
        p = z + 5
        for c in range(3):
            b[c, p, 0:4] = y_low[z, 4 * c : 4 * c + 4]
            b[c, p, 4:20] = load[c, z]
            b[c, p, 20:24] = y_high[z, 4 * c : 4 * c + 4]
        m[p, 0:4] = y_low[z, 12:16]
        m[p, 4:20] = m_own[z]
        m[p, 20:24] = y_high[z, 12:16]
        k[p, 0:8] = y_low[z, 16:24]
        k[p, 8:24] = k_own[z]
        k[p, 24:32] = y_high[z, 16:24]
    for src, high in ((partner.at[1 - odd], 1 - odd), (cross, odd)):
        start, k_start = 1 + 20 * high, 21 * high
        for q in range(4):
            for a in range(4):
                part = src[24 * (4 * a + q) : 24 * (4 * a + q) + 24]
                if a < 3:
                    b[a, start + q] = part
                else:
                    m[start + q] = part
        for q in range(5):
            k[k_start + q] = src[384 + 32 * q : 416 + 32 * q]
    fine_coefficients(k, m, co, (1, 25))
    first_sweep((1, 25), b, first, w)
    sweep((2, 24), b, first, u, k, co, 1, FINE)

    def coarse_k(n, q):
        p = 2 * n + 3
        k1[n] = block_mean(k[p], k[p + 1], tmp.at[q], 1)

    loop(0, 10, coarse_k, 5)
    lane = lanes_of(8)
    odd_lane = (lane & 1) != 0
    lane = lanes_of(16)

    def down(z1, s):
        p = 2 * z1 + 5
        rests = [left_over(q, b, u, k, co, 1, FINE)[1] for q in (p, p + 1)]
        parts = [
            block_mean(m[p] * rests[0][c], m[p + 1] * rests[1][c], tmp.at[3 * s + c], 1)[2:10] for c in range(3)
        ]
        centre = k1[z1 + 1]
        sides = jnp.where(lane < 126, lane_next(centre, 2), 0.0) + jnp.where(lane >= 2, lane_prev(centre, 2), 0.0)
        total = 0.125 * (6.0 * centre + sides + row_next(centre) + row_prev(centre) + k1[z1] + k1[z1 + 2])
        message[z1] = jnp.where(odd_lane, parts[1], parts[0])
        message[8 + z1] = jnp.where(odd_lane, centre[4:12], parts[2])
        sums[z1] = total[4:12]

    loop(0, 8, down, 4)
    for z1 in range(4):
        message[16 + z1] = jnp.where(odd_lane, sums[z1 + 4], sums[z1])


def middle_kernel(place, own, partner, cross,
                  b1_out, u1_out, k1_out, t1_out, b2, k2, u2b, packed, co2_out,
                  b1, u1, k1, t1, cx, cy, cz, e, w, first, u2a, tmp):
    co = (cx, cy, cz, e, w)
    lane = lanes_of(24)
    odd_lane = (lane & 1) != 0
    odd = place[0] & 1
    for src, start in ((own, 8), (partner.at[1 - odd], 16 * (1 - odd)), (cross, 16 * odd)):
        for q in range(8):
            p = start + q
            v = src[q]
            b1[0, p] = jnp.where(odd_lane, lane_prev(v, 1), v)
            b1[1, p] = jnp.where(odd_lane, v, lane_next(v, 1))
            v = src[8 + q]
            b1[2, p] = jnp.where(odd_lane, lane_prev(v, 1), v)
            k1[p] = jnp.where(odd_lane, v, lane_next(v, 1))
        for q in range(4):
            v = src[16 + q]
            t1[start + q] = jnp.where(odd_lane, lane_prev(v, 1), v)
            t1[start + 4 + q] = jnp.where(odd_lane, v, lane_next(v, 1))
    k1[24] = jnp.zeros((24, 128), F32)

    def fill(p):
        for ref, v in zip(co, coefficients(k1[p], None, k1[p + 1], 0.25, 2, None, t1[p])):
            ref[p] = v
        for c in range(3):
            first[c, p] = w[p] * b1[c, p]

    each((0, 24), fill)
    sweep((1, 23), b1, first, u1, k1, co, 2)
    def keep(p):
        k1_out[p] = k1[p + 4, 4:20]
        t1_out[p] = t1[p + 4, 4:20]
        for c in range(3):
            b1_out[c, p] = b1[c, p + 4, 4:20]
            u1_out[c, p] = u1[c, p + 4, 4:20]

    each((0, 16), keep)

    def coarse_k(q2, s):
        k2[q2, 4:16] = block_mean(k1[2 * q2], k1[2 * q2 + 1], tmp.at[s], 2)
        k2[q2, 0:4] = jnp.zeros((4, 128), F32)

    loop(0, 12, coarse_k, 6)

    def down(q2, s):
        rests = [left_over(p, b1, u1, k1, co, 2)[1] for p in (2 * q2, 2 * q2 + 1)]
        for c in range(3):
            b2[c, q2, 4:16] = block_mean(rests[0][c], rests[1][c], tmp.at[3 * s + c], 2)
            b2[c, q2, 0:4] = jnp.zeros((4, 128), F32)

    loop(1, 11, down, 5)
    co2 = tuple(co2_out.at[n] for n in range(5))
    fill_coefficients(k2, co2, (1, 11), 0.0625, 4)
    co2[2][0] = (0.5 * 0.0625) * (k2[0] + k2[1])
    first_sweep((1, 11), b2, u2a, co2[4])
    sweep((2, 10), b2, u2a, u2b, k2, co2, 4)
    j = place[0] // 2
    lane = lanes_of(8)
    group = lane & 7
    pack = jnp.zeros((8, 128), F32)
    for zz in range(2):
        rests = [left_over(p, b2, u2b, k2, co2, 4)[1] for p in (4 + 2 * zz, 5 + 2 * zz)]
        parts = [block_mean(rests[0][c], rests[1][c], tmp.at[4 * zz + c], 4) for c in range(3)]
        parts.append(block_mean(k2[4 + 2 * zz], k2[5 + 2 * zz], tmp.at[4 * zz + 3], 4))
        for a in range(4):
            pack = jnp.where(group == ((j + 2 * a + zz) & 7), parts[a], pack)
    quad = lane & 3
    low, high = tmp.at[8], tmp.at[9]
    low[0:2] = pack[4:6]
    high[0:2] = pack[4:6]
    for c in range(3):
        v = u2b[c, 7, 8:16]
        for zz in (2, 1, 0):
            v = jnp.where(quad == zz, u2b[c, 4 + zz, 8:16], v)
        low[2 + 2 * c : 4 + 2 * c] = v[2:4]
        high[2 + 2 * c : 4 + 2 * c] = v[0:2]
    to_low, to_high = low[0:8], high[0:8]
    for peer in range(COL):
        packed[peer] = jnp.where(place[1] < peer, to_high, to_low)


def window_kernel(place, received, u2, out, tmp):
    c, d = place[1], place[0]
    for q in range(11):
        peer = c - 5 + q
        inside = jnp.logical_and(peer >= 0, peer < COL).astype(F32)
        tmp[2 * q : 2 * q + 2] = inside * received[jnp.clip(peer, 0, COL - 1), 0:2]
    for comp in range(3):
        for q, peer in ((0, c - 1), (1, c + 1)):
            inside = jnp.logical_and(peer >= 0, peer < COL).astype(F32)
            part = received[jnp.clip(peer, 0, COL - 1), 2 + 2 * comp : 4 + 2 * comp]
            base = 22 + 4 * comp + 2 * q
            tmp[base : base + 2] = inside * part
    quad = lanes_of(4) & 3
    tmp[46:48] = jnp.zeros((2, 128), F32)

    def inner(near):
        for comp in range(3):
            a = [u2[comp, 4 + near + f, 6:10] for f in range(2)]
            b = [u2[comp, 4 + near + f, 10:14] for f in range(2)]
            v = jnp.where(quad == 0, a[0], jnp.where(quad == 1, a[1], jnp.where(quad == 2, b[0], b[1])))
            tmp[34 + 4 * comp : 38 + 4 * comp] = v
        return tmp[...]

    to_high = inner(0)
    to_low = inner(2)
    for q in range(SLAB // 2):
        out[q] = jnp.where(q + 1 - (d & 1) > d // 2, to_high, to_low)


def upper_kernel(place, received, u2, b2, k2, co2, b1, u1, k1, t1, b0, u0, k0, m0, co0,
                 field, residual,
                 b3, k3, co3, u3a, u3b, u2a, u2b, co1, u1a, u1b, u0a, u0b, tmp):
    d = place[0]
    lane = lanes_of(24)
    group = lane & 7

    def unpack(a, carry):
        mixes = [jnp.zeros((24, 128), F32)] * 8
        for j in range(8):
            v = received[a, j, 0:24]
            for r in range(8):
                mixes[r] = jnp.where(group == ((j + r) & 7), v, mixes[r])
        for r in range(8):
            mix = mixes[r]
            if r:
                mix = jnp.where(group < 8 - r, lane_next(mix, r), lane_prev(mix, 8 - r))
            arr, plane = r // 2, 2 * a + r % 2
            if arr < 3:
                b3[arr, plane] = mix
            else:
                k3[plane] = mix
        return carry

    lax.fori_loop(0, 2, unpack, 0)

    def above(v_of, i):
        return v_of(i + 1) if i < 3 else jnp.where(group < 7, lane_next(v_of(0), 1), 0.0)

    def below(v_of, i):
        return v_of(i - 1) if i > 0 else jnp.where(group > 0, lane_prev(v_of(3), 1), 0.0)

    cx3, cy3, cz3, e3, w3 = (co3.at[n] for n in range(5))
    for i in range(4):
        cx, cy, cz, e, w = coefficients(
            k3[i], below(lambda q: k3[q], i), above(lambda q: k3[q], i), 1.0 / 64.0, 8, None
        )
        cx3[i] = cx
        cy3[i] = cy
        cz3[i] = cz
        e3[i] = e
        w3[i] = w
        for c in range(3):
            u3a[c, i] = w * b3[c, i]

    def coarse(src, dst):
        for i in range(4):
            u = [src[c, i] for c in range(3)]
            lo = [below(lambda q: src[c, q], i) for c in range(3)]
            hi = [above(lambda q: src[c, q], i) for c in range(3)]
            b = [b3[c, i] for c in range(3)]
            cz_lo = below(lambda q: cz3[q], i)
            rest = remainder(b, u, lo, hi, k3[i], cx3[i], cy3[i], cz3[i], cz_lo, e3[i], 8)
            for c in range(3):
                dst[c, i] = u[c] + w3[i] * rest[c]

    def two(t, carry):
        coarse(u3a, u3b)
        coarse(u3b, u3a)
        return carry

    lax.fori_loop(0, 3, two, 0)
    coarse(u3a, u3b)

    c2 = tuple(co2.at[n] for n in range(5))
    lane8 = lanes_of(8)
    lane4 = lanes_of(4)

    def outer(g, carry):
        peer = d - 1 + g
        inside = jnp.logical_and(peer >= 0, peer < SLAB)
        peer = jnp.clip(peer, 0, SLAB - 1)
        for zz in range(4):
            pick = jnp.logical_and((lane4 & 3) == zz, inside)
            for c in range(3):
                v = spread(jnp.where(pick, received[peer & 1, peer // 2, 22 + 4 * c : 26 + 4 * c], 0.0), lane4, 4)
                u2a[c, 4 * g + zz, 0:4] = jnp.zeros((4, 128), F32)
                u2a[c, 4 * g + zz, 4:6] = v[0:2]
                u2a[c, 4 * g + zz, 14:16] = v[2:4]
        return carry

    lax.fori_loop(0, 3, outer, 0)

    def middle(q2, _):
        for c in range(3):
            u2a[c, q2, 6:14] = u2[c, q2, 6:14]

    loop(2, 10, middle, 4)

    def far(g, carry):
        peer = d - 1 + 2 * g
        inside = jnp.logical_and(peer >= 0, peer < SLAB)
        peer = jnp.clip(peer, 0, SLAB - 1)
        for c in range(3):
            v = received[peer & 1, peer // 2, 34 + 4 * c : 38 + 4 * c]
            for f in range(2):
                for half in range(2):
                    pick = jnp.logical_and((lane4 & 3) == 2 * half + f, inside)
                    u2a[c, 10 * g + f, 6 + 4 * half : 10 + 4 * half] = spread(jnp.where(pick, v, 0.0), lane4, 4)
        return carry

    lax.fori_loop(0, 2, far, 0)

    def add_coarse(t, s):
        z = 2 * d - 2 + t
        i = (z + 32) & 3
        j = z >> 2
        for c in range(3):
            v = jnp.where((lane8 & 7) == j, u3b[c, i, 8:16], 0.0)
            double_rows(spread(v, lane8, 8), tmp.at[3 * s + c])
            for q2 in (2 * t, 2 * t + 1):
                u2a[c, q2, 4:16] = u2a[c, q2, 4:16] + tmp[3 * s + c, 0:12]

    loop(0, 6, add_coarse, 3)
    sweep((1, 11), b2, u2a, u2b, k2, c2, 4)
    sweep((2, 10), b2, u2b, u2a, k2, c2, 4)

    c1 = tuple(co1.at[n] for n in range(5))

    def fill(p):
        for ref, v in zip(c1, coefficients(k1[p], None, k1[p + 1], 0.25, 2, None, t1[p])):
            ref[p] = v

    each((0, 15), fill)

    def add_middle(q2, s):
        for c in range(3):
            double_rows(u2a[c, q2, 6:14], tmp.at[3 * s + c])
            more = tmp[3 * s + c, 0:16]
            for p in (2 * q2 - 4, 2 * q2 - 3):
                u1a[c, p] = u1[c, p] + more

    loop(2, 10, add_middle, 4)
    sweep((1, 15), b1, u1a, u1b, k1, c1, 2)
    sweep((2, 14), b1, u1b, u1a, k1, c1, 2)

    c0 = tuple(co0.at[n] for n in range(5))
    def add_fine(p1, s):
        for c in range(3):
            double_rows(u1a[c, p1], tmp.at[3 * s + c])
            more = tmp[3 * s + c, 4:28]
            for p in (2 * p1 - 3, 2 * p1 - 2):
                u0a[c, p] = u0[c, p] + m0[p] * more

    loop(2, 14, add_fine, 4)
    sweep((3, 23), b0, u0a, u0b, k0, c0, 1, FINE)
    sweep((4, 22), b0, u0b, u0a, k0, c0, 1, FINE)

    def last(z):
        p = z + 5
        u, rest = left_over(p, b0, u0a, k0, c0, 1, FINE)
        for c in range(3):
            field[c, z] = u[c][4:20]
            residual[c, z] = (m0[p] * rest[c])[4:20]

    each((0, 16), last)


def struct(*shape):
    return jax.ShapeDtypeStruct(shape, F32)


def call(kernel, name, outs, scratch, *args, smem=0):
    vmem = pl.BlockSpec(memory_space=pltpu.VMEM)
    specs = [pl.BlockSpec(memory_space=pltpu.SMEM)] * smem
    return pl.pallas_call(
        kernel,
        name=name,
        out_shape=outs,
        in_specs=specs + [vmem] * (len(args) - len(specs)),
        out_specs=jax.tree.map(lambda _: vmem, outs),
        scratch_shapes=[pltpu.VMEM(s, F32) for s in scratch],
        compiler_params=pltpu.CompilerParams(vmem_limit_bytes=40 * 1024 * 1024),
    )(*args)


def shift(block, axis, count, by):
    pairs = [(i, i + by) for i in range(count) if 0 <= i + by < count]
    return lax.ppermute(block, axis, pairs)


def slab_neighbours(to_partner, to_cross):
    pairs = []
    for i in range(1, SLAB - 1, 2):
        pairs += [(i, i + 1), (i + 1, i)]
    cross = lax.ppermute(to_cross, "slab", pairs)
    groups = [[i, i + 1] for i in range(0, SLAB, 2)]
    return lax.all_gather(to_partner, "slab", axis_index_groups=groups), cross


def on_device(load, density, moduli, fixed):
    place = jnp.stack([lax.axis_index("slab"), lax.axis_index("col")]).astype(jnp.int32)
    own = struct(16, 16, 128)
    raw = jnp.concatenate([load, density[None].astype(F32), fixed[None].astype(F32)], axis=0)
    k, m, low, high = call(
        prep_kernel, "prep", (own, own, struct(16, 24, 128), struct(16, 24, 128)), [], moduli, raw, smem=1
    )
    y_low = shift(high, "col", COL, 1)
    y_high = shift(low, "col", COL, -1)
    to_partner, to_cross = call(
        planes_kernel, "planes", (struct(544, 128), struct(544, 128)), [],
        place, raw, k, m, y_low, y_high, smem=1,
    )
    partner, cross = slab_neighbours(to_partner, to_cross)
    part0, full0, full0v = (26, 24, 128), (26, 32, 128), (3, 26, 24, 128)
    b0, u0, k0, m0, message, co0 = call(
        fine_kernel, "fine",
        (struct(*full0v), struct(*full0v), struct(*full0), struct(*part0), struct(20, 8, 128),
         struct(5, *part0)),
        [full0v, (10, 16, 128), (8, 8, 128), (16, 48, 128)],
        place, raw, k, m, y_low, y_high, partner, cross, smem=1,
    )
    y_low = shift(message, "col", COL, 1)
    y_high = shift(message, "col", COL, -1)
    wide = jnp.concatenate([y_low, message, y_high], axis=1)
    partner, cross = slab_neighbours(wide, wide)
    full1, full1v, more1 = (24, 24, 128), (3, 24, 24, 128), (25, 24, 128)
    part1, part1v = (16, 16, 128), (3, 16, 16, 128)
    full2, full2v = (12, 16, 128), (3, 12, 16, 128)
    b1, u1, k1, t1, b2, k2, u2, packed, co2 = call(
        middle_kernel, "middle",
        (struct(*part1v), struct(*part1v), struct(*part1), struct(*part1), struct(*full2v), struct(*full2),
         struct(*full2v), struct(COL, 8, 128), struct(5, *full2)),
        [full1v, full1v, more1, full1] + [full1] * 5 + [full1v] + [full2v, (16, 48, 128)],
        place, wide, partner, cross, smem=1,
    )
    received = lax.all_to_all(packed, "col", 0, 0)
    window = call(window_kernel, "window", struct(SLAB // 2, 48, 128), [(48, 128)], place, received, u2, smem=1)
    groups = [list(range(par, SLAB, 2)) for par in range(2)]
    received = lax.all_to_all(window, "slab", 0, 0, axis_index_groups=groups)
    received = lax.all_gather(received, "slab", axis_index_groups=[[i, i + 1] for i in range(0, SLAB, 2)])
    full3, full3v = (4, 24, 128), (3, 4, 24, 128)
    return call(
        upper_kernel, "upper",
        (struct(3, 16, 16, 128), struct(3, 16, 16, 128)),
        [full3v, full3, (5,) + full3, full3v, full3v, full2v, full2v,
         (5,) + part1, part1v, part1v, full0v, full0v, (16, 48, 128)],
        place, received, u2, b2, k2, co2, b1, u1, k1, t1, b0, u0, k0, m0, co0, smem=1,
    )


def solution(mesh):
    placed = (P(None, "slab", "col", None), P("slab", "col", None), P(), P("slab", "col", None))
    return jax.shard_map(
        on_device,
        mesh=mesh,
        in_specs=placed,
        out_specs=(P(None, "slab", "col", None), P(None, "slab", "col", None)),
        check_vma=False,
    )
```

```python
import jax
import jax.numpy as jnp
from jax import lax
from jax.experimental import pallas as pl
from jax.experimental.pallas import tpu as pltpu
from jax.sharding import PartitionSpec as P

CLASSES = 8
OMEGA = 0.6
COUPLE = 0.05
SLAB = 16
COL = 32
F32 = jnp.float32


def loop(low, high, body, unroll):
    def step(t, carry):
        for q in range(unroll):
            body(low + t * unroll + q, q)
        return carry

    assert (high - low) % unroll == 0
    lax.fori_loop(0, (high - low) // unroll, step, 0)


def span(low, count, body, unroll=None):
    fits = [n for n in (8, 7, 6, 5, 4, 11, 3, 2) if count % n == 0]
    loop(0, count, lambda n, q: body(low + n, q), unroll or fits[0])


def each(planes, body):
    count = planes[2] if len(planes) == 3 else planes[1] - planes[0]
    span(planes[0], count, lambda p, q: body(p))


def lanes_of(rows):
    return lax.broadcasted_iota(jnp.int32, (rows, 128), 1)


def lane_next(v, step):
    return pltpu.roll(v, 128 - step, 1)


def lane_prev(v, step):
    return pltpu.roll(v, step, 1)


def row_next(v):
    return pltpu.roll(v, v.shape[0] - 1, 0)


def row_prev(v):
    return pltpu.roll(v, 1, 0)


def spread(v, lane, width):
    step = 1
    while step < width:
        v = v + jnp.where((lane & step) != 0, lane_prev(v, step), lane_next(v, step))
        step *= 2
    return v


def coefficients(k, k_lo, k_hi, scale, step, mask, total=None):
    lane = lanes_of(k.shape[0])
    half = 0.5 * scale
    k_next = lane_next(k, step)
    cx = jnp.where(lane < 128 - step, half * (k + k_next), 0.0)
    ky = row_next(k)
    cy = half * (k + ky)
    cz = half * (k + k_hi)
    if total is None:
        sides = jnp.where(lane < 128 - step, k_next, 0.0) + jnp.where(lane >= step, lane_prev(k, step), 0.0)
        total = half * (6.0 * k + sides + ky + row_prev(k) + k_lo + k_hi)
    diag = total + 2.0 * COUPLE * k
    top = OMEGA if mask is None else OMEGA * mask
    weight = jnp.where(k > 0.0, top / diag, 0.0)
    return cx, cy, cz, total + COUPLE * k, weight


def remainder(b, u, u_lo, u_hi, k, cx, cy, cz, cz_lo, e, step):
    cx_lo = lane_prev(cx, step)
    cy_lo = row_prev(cy)
    shared = COUPLE * k * (u[0] + u[1] + u[2])
    out = []
    for c in range(3):
        v = u[c]
        around = cx * lane_next(v, step) + cx_lo * lane_prev(v, step)
        around = around + cy * row_next(v) + cy_lo * row_prev(v)
        around = around + cz * u_hi[c] + cz_lo * u_lo[c]
        out.append((b[c] - shared) + (around - e * v))
    return out


def fill_coefficients(k_ref, co, planes, scale, step, total_ref=None):
    def body(p):
        total = None if total_ref is None else total_ref[p]
        values = coefficients(k_ref[p], k_ref[p - 1], k_ref[p + 1], scale, step, None, total)
        for ref, v in zip(co, values):
            ref[p] = v

    each(planes, body)


def fine_coefficients(k_ref, m_ref, co, planes):
    def body(p):
        k = k_ref[p, 4:28]
        k_lo, k_hi = k_ref[p - 1, 4:28], k_ref[p + 1, 4:28]
        ky, ky_lo = k_ref[p, 5:29], k_ref[p, 3:27]
        lane = lanes_of(24)
        k_next = jnp.where(lane < 127, lane_next(k, 1), 0.0)
        k_prev = jnp.where(lane >= 1, lane_prev(k, 1), 0.0)
        total = 0.5 * (6.0 * k + k_next + k_prev + ky + ky_lo + k_lo + k_hi)
        values = (
            jnp.where(lane < 127, 0.5 * (k + k_next), 0.0), 0.5 * (k + ky), 0.5 * (k + k_hi),
            total + COUPLE * k,
            jnp.where(k > 0.0, OMEGA * m_ref[p] / (total + 2.0 * COUPLE * k), 0.0),
        )
        for ref, v in zip(co, values):
            ref[p] = v

    each(planes, body)


def left_over(p, b_ref, u_ref, k_ref, co, step, rows=slice(None)):
    cx_ref, cy_ref, cz_ref, e_ref, _ = co
    b = [b_ref[c, p] for c in range(3)]
    u = [u_ref[c, p] for c in range(3)]
    lo = [u_ref[c, p - 1] for c in range(3)]
    hi = [u_ref[c, p + 1] for c in range(3)]
    k = k_ref[p, rows]
    return u, remainder(b, u, lo, hi, k, cx_ref[p], cy_ref[p], cz_ref[p], cz_ref[p - 1], e_ref[p], step)


def sweep(planes, b_ref, u_ref, new_ref, k_ref, co, step, rows=slice(None)):
    def body(p):
        u, rest = left_over(p, b_ref, u_ref, k_ref, co, step, rows)
        w = co[4][p]
        for c in range(3):
            new_ref[c, p] = u[c] + w * rest[c]

    each(planes, body)


def first_sweep(planes, b_ref, new_ref, w_ref):
    def body(p):
        w = w_ref[p]
        for c in range(3):
            new_ref[c, p] = w * b_ref[c, p]

    each(planes, body)


def block_mean(a, b, tmp, step):
    lane = lanes_of(a.shape[0])
    s = a + b
    s = s + jnp.where((lane & step) != 0, lane_prev(s, step), lane_next(s, step))
    n = a.shape[0]
    tmp[0:n] = s
    return 0.125 * (tmp[pl.ds(0, n // 2, stride=2)] + tmp[pl.ds(1, n // 2, stride=2)])


def double_rows(v, tmp):
    n = v.shape[0]
    tmp[pl.ds(0, n, stride=2)] = v
    tmp[pl.ds(1, n, stride=2)] = v


FINE = slice(4, 28)


def prep_kernel(moduli, raw, k_out, m_out, low, high):
    def body(z):
        d = raw[3, z]
        k = jnp.zeros((16, 128), F32)
        for klass in range(CLASSES):
            k = jnp.where(d == float(klass), moduli[klass], k)
        m = 1.0 - raw[4, z]
        k_out[z] = k
        m_out[z] = m
        for c in range(3):
            low[z, 4 * c : 4 * c + 4] = raw[c, z, 0:4]
            high[z, 4 * c : 4 * c + 4] = raw[c, z, 12:16]
        low[z, 12:16] = m[0:4]
        high[z, 12:16] = m[12:16]
        low[z, 16:24] = k[0:8]
        high[z, 16:24] = k[8:16]

    each((0, 16), body)


def planes_kernel(place, load, k, m, from_low, from_high, partner, cross):
    odd = place[0] & 1
    for out, start, k_start in (
        (partner, 12 * (1 - odd), 11 * (1 - odd)), (cross, 12 * odd, 11 * odd),
    ):
        for q in range(4):
            z = start + q
            for a in range(4):
                base = 24 * (4 * a + q)
                own = load[a, z] if a < 3 else m[z]
                out[base : base + 4] = from_low[z, 4 * a : 4 * a + 4]
                out[base + 4 : base + 20] = own
                out[base + 20 : base + 24] = from_high[z, 4 * a : 4 * a + 4]
        for q in range(5):
            z = k_start + q
            base = 384 + 32 * q
            out[base : base + 8] = from_low[z, 16:24]
            out[base + 8 : base + 24] = k[z]
            out[base + 24 : base + 32] = from_high[z, 16:24]


def fine_part(odd, near, b, u, k, m, message, co_out, first, k1, sums, tmp):
    co = tuple(co_out.at[n] for n in range(5))
    even = 1 - odd
    if near:
        (c_low, c_count), (s_low, s_count) = (1 + 6 * even, 18), (2 + 6 * even, 16)
        (k_low, k_count), (d_low, d_count) = (2 * even, 8), (2 * even, 6)
    else:
        (c_low, c_count), (s_low, s_count) = (1 + 18 * odd, 6), (2 + 16 * odd, 6)
        (k_low, k_count), (d_low, d_count) = (8 * odd, 2), (6 * odd, 2)
    fine_coefficients(k, m, co, (c_low, None, c_count))
    first_sweep((c_low, None, c_count), b, first, co[4])
    sweep((s_low, None, s_count), b, first, u, k, co, 1, FINE)

    def coarse_k(n, q):
        p = 2 * n + 3
        k1[n] = block_mean(k[p], k[p + 1], tmp.at[q], 1)

    span(k_low, k_count, coarse_k)
    lane = lanes_of(8)
    odd_lane = (lane & 1) != 0
    lane = lanes_of(16)

    def down(z1, s):
        p = 2 * z1 + 5
        rests = [left_over(q, b, u, k, co, 1, FINE)[1] for q in (p, p + 1)]
        parts = [
            block_mean(m[p] * rests[0][c], m[p + 1] * rests[1][c], tmp.at[3 * s + c], 1)[2:10] for c in range(3)
        ]
        centre = k1[z1 + 1]
        sides = jnp.where(lane < 126, lane_next(centre, 2), 0.0) + jnp.where(lane >= 2, lane_prev(centre, 2), 0.0)
        total = 0.125 * (6.0 * centre + sides + row_next(centre) + row_prev(centre) + k1[z1] + k1[z1 + 2])
        message[z1] = jnp.where(odd_lane, parts[1], parts[0])
        message[8 + z1] = jnp.where(odd_lane, centre[4:12], parts[2])
        sums[z1] = total[4:12]

    span(d_low, d_count, down, 3 if near else 2)


def place_planes(src, high, b, m, k):
    start, k_start = 1 + 20 * high, 21 * high
    for q in range(4):
        for a in range(4):
            part = src[24 * (4 * a + q) : 24 * (4 * a + q) + 24]
            if a < 3:
                b[a, start + q] = part
            else:
                m[start + q] = part
    for q in range(5):
        k[k_start + q] = src[384 + 32 * q : 416 + 32 * q]


def fine_near_kernel(place, load, k_own, m_own, y_low, y_high, partner, *refs):
    b, u, k, m, message, co_out, first, k1, sums, tmp = refs
    odd = place[0] & 1

    def own(z):
        p = z + 5
        for c in range(3):
            b[c, p, 0:4] = y_low[z, 4 * c : 4 * c + 4]
            b[c, p, 4:20] = load[c, z]
            b[c, p, 20:24] = y_high[z, 4 * c : 4 * c + 4]
        m[p, 0:4] = y_low[z, 12:16]
        m[p, 4:20] = m_own[z]
        m[p, 20:24] = y_high[z, 12:16]
        k[p, 0:8] = y_low[z, 16:24]
        k[p, 8:24] = k_own[z]
        k[p, 24:32] = y_high[z, 16:24]

    each((0, 16), own)
    place_planes(partner.at[1 - odd], 1 - odd, b, m, k)
    fine_part(odd, True, *refs)


def fine_far_kernel(place, cross, *refs):
    refs = refs[9:]
    b, u, k, m, message, co_out, first, k1, sums, tmp = refs
    odd = place[0] & 1
    place_planes(cross, odd, b, m, k)
    fine_part(odd, False, *refs)
    odd_lane = (lanes_of(8) & 1) != 0
    for z1 in range(4):
        message[16 + z1] = jnp.where(odd_lane, sums[z1 + 4], sums[z1])


def middle_part(odd, near, b1, u1, k1, t1, co_out, first, b2, k2, tmp):
    co = tuple(co_out.at[n] for n in range(5))
    even = 1 - odd
    if near:
        (c_low, c_count), (s_low, s_count) = (8 * even, 16), (1 + 8 * even, 14)
        (k_low, k_count), (d_low, d_count) = (4 * even, 8), (1 + 4 * even, 6)
    else:
        (c_low, c_count), (s_low, s_count) = (15 * odd, 9), (1 + 14 * odd, 8)
        (k_low, k_count), (d_low, d_count) = (8 * odd, 4), (1 + 6 * odd, 4)

    def fill(p):
        for ref, v in zip(co, coefficients(k1[p], None, k1[p + 1], 0.25, 2, None, t1[p])):
            ref[p] = v
        for c in range(3):
            first[c, p] = co[4][p] * b1[c, p]

    each((c_low, None, c_count), fill)
    sweep((s_low, None, s_count), b1, first, u1, k1, co, 2)

    def coarse_k(q2, s):
        k2[q2, 4:16] = block_mean(k1[2 * q2], k1[2 * q2 + 1], tmp.at[s], 2)
        k2[q2, 0:4] = jnp.zeros((4, 128), F32)

    span(k_low, k_count, coarse_k, 4)

    def down(q2, s):
        rests = [left_over(p, b1, u1, k1, co, 2)[1] for p in (2 * q2, 2 * q2 + 1)]
        for c in range(3):
            b2[c, q2, 4:16] = block_mean(rests[0][c], rests[1][c], tmp.at[3 * s + c], 2)
            b2[c, q2, 0:4] = jnp.zeros((4, 128), F32)

    span(d_low, d_count, down, 3 if near else 4)


def take(src, start, b1, k1, t1):
    odd_lane = (lanes_of(24) & 1) != 0
    for q in range(8):
        p = start + q
        v = src[q]
        b1[0, p] = jnp.where(odd_lane, lane_prev(v, 1), v)
        b1[1, p] = jnp.where(odd_lane, v, lane_next(v, 1))
        v = src[8 + q]
        b1[2, p] = jnp.where(odd_lane, lane_prev(v, 1), v)
        k1[p] = jnp.where(odd_lane, v, lane_next(v, 1))
    for q in range(4):
        v = src[16 + q]
        t1[start + q] = jnp.where(odd_lane, lane_prev(v, 1), v)
        t1[start + 4 + q] = jnp.where(odd_lane, v, lane_next(v, 1))


def middle_near_kernel(place, own, partner, *refs):
    b1, u1, k1, t1 = refs[:4]
    odd = place[0] & 1
    take(own, 8, b1, k1, t1)
    take(partner.at[1 - odd], 16 * (1 - odd), b1, k1, t1)
    k1[24] = jnp.zeros((24, 128), F32)
    middle_part(odd, True, *refs)


def middle_far_kernel(place, cross, *refs):
    refs = refs[8:]
    b1, u1, k1, t1, co_out, first, b2, k2 = refs[:8]
    b1_out, u1_out, k1_out, t1_out, u2b, packed, co2_out, u2a, tmp = refs[8:]
    odd = place[0] & 1
    take(cross, 16 * odd, b1, k1, t1)
    middle_part(odd, False, b1, u1, k1, t1, co_out, first, b2, k2, tmp)

    def keep(p):
        k1_out[p] = k1[p + 4, 4:20]
        t1_out[p] = t1[p + 4, 4:20]
        for c in range(3):
            b1_out[c, p] = b1[c, p + 4, 4:20]
            u1_out[c, p] = u1[c, p + 4, 4:20]

    each((0, 16), keep)
    co2 = tuple(co2_out.at[n] for n in range(5))
    fill_coefficients(k2, co2, (1, 11), 0.0625, 4)
    co2[2][0] = (0.5 * 0.0625) * (k2[0] + k2[1])
    first_sweep((1, 11), b2, u2a, co2[4])
    sweep((2, 10), b2, u2a, u2b, k2, co2, 4)
    j = place[0] // 2
    lane = lanes_of(8)
    group = lane & 7
    pack = jnp.zeros((8, 128), F32)
    for zz in range(2):
        rests = [left_over(p, b2, u2b, k2, co2, 4)[1] for p in (4 + 2 * zz, 5 + 2 * zz)]
        parts = [block_mean(rests[0][c], rests[1][c], tmp.at[4 * zz + c], 4) for c in range(3)]
        parts.append(block_mean(k2[4 + 2 * zz], k2[5 + 2 * zz], tmp.at[4 * zz + 3], 4))
        for a in range(4):
            pack = jnp.where(group == ((j + 2 * a + zz) & 7), parts[a], pack)
    quad = lane & 3
    low, high = tmp.at[8], tmp.at[9]
    low[0:2] = pack[4:6]
    high[0:2] = pack[4:6]
    for c in range(3):
        v = u2b[c, 7, 8:16]
        for zz in (2, 1, 0):
            v = jnp.where(quad == zz, u2b[c, 4 + zz, 8:16], v)
        low[2 + 2 * c : 4 + 2 * c] = v[2:4]
        high[2 + 2 * c : 4 + 2 * c] = v[0:2]
    to_low, to_high = low[0:8], high[0:8]
    for peer in range(COL):
        packed[peer] = jnp.where(place[1] < peer, to_high, to_low)


def window_kernel(place, received, u2, out, tmp):
    c, d = place[1], place[0]
    for q in range(11):
        peer = c - 5 + q
        inside = jnp.logical_and(peer >= 0, peer < COL).astype(F32)
        tmp[2 * q : 2 * q + 2] = inside * received[jnp.clip(peer, 0, COL - 1), 0:2]
    for comp in range(3):
        for q, peer in ((0, c - 1), (1, c + 1)):
            inside = jnp.logical_and(peer >= 0, peer < COL).astype(F32)
            part = received[jnp.clip(peer, 0, COL - 1), 2 + 2 * comp : 4 + 2 * comp]
            base = 22 + 4 * comp + 2 * q
            tmp[base : base + 2] = inside * part
    quad = lanes_of(4) & 3
    tmp[46:48] = jnp.zeros((2, 128), F32)

    def inner(near):
        for comp in range(3):
            a = [u2[comp, 4 + near + f, 6:10] for f in range(2)]
            b = [u2[comp, 4 + near + f, 10:14] for f in range(2)]
            v = jnp.where(quad == 0, a[0], jnp.where(quad == 1, a[1], jnp.where(quad == 2, b[0], b[1])))
            tmp[34 + 4 * comp : 38 + 4 * comp] = v
        return tmp[...]

    to_high = inner(0)
    to_low = inner(2)
    for q in range(SLAB // 2):
        out[q] = jnp.where(q + 1 - (d & 1) > d // 2, to_high, to_low)


def upper_kernel(place, received, u2, b2, k2, co2, b1, u1, k1, t1, b0, u0, k0, m0, co0,
                 field, residual,
                 b3, k3, co3, u3a, u3b, u2a, u2b, co1, u1a, u1b, u0a, u0b, tmp):
    d = place[0]
    lane = lanes_of(24)
    group = lane & 7

    def unpack(a, carry):
        mixes = [jnp.zeros((24, 128), F32)] * 8
        for j in range(8):
            v = received[a, j, 0:24]
            for r in range(8):
                mixes[r] = jnp.where(group == ((j + r) & 7), v, mixes[r])
        for r in range(8):
            mix = mixes[r]
            if r:
                mix = jnp.where(group < 8 - r, lane_next(mix, r), lane_prev(mix, 8 - r))
            arr, plane = r // 2, 2 * a + r % 2
            if arr < 3:
                b3[arr, plane] = mix
            else:
                k3[plane] = mix
        return carry

    lax.fori_loop(0, 2, unpack, 0)

    def above(v_of, i):
        return v_of(i + 1) if i < 3 else jnp.where(group < 7, lane_next(v_of(0), 1), 0.0)

    def below(v_of, i):
        return v_of(i - 1) if i > 0 else jnp.where(group > 0, lane_prev(v_of(3), 1), 0.0)

    cx3, cy3, cz3, e3, w3 = (co3.at[n] for n in range(5))
    for i in range(4):
        cx, cy, cz, e, w = coefficients(
            k3[i], below(lambda q: k3[q], i), above(lambda q: k3[q], i), 1.0 / 64.0, 8, None
        )
        cx3[i] = cx
        cy3[i] = cy
        cz3[i] = cz
        e3[i] = e
        w3[i] = w
        for c in range(3):
            u3a[c, i] = w * b3[c, i]

    def coarse(src, dst):
        for i in range(4):
            u = [src[c, i] for c in range(3)]
            lo = [below(lambda q: src[c, q], i) for c in range(3)]
            hi = [above(lambda q: src[c, q], i) for c in range(3)]
            b = [b3[c, i] for c in range(3)]
            cz_lo = below(lambda q: cz3[q], i)
            rest = remainder(b, u, lo, hi, k3[i], cx3[i], cy3[i], cz3[i], cz_lo, e3[i], 8)
            for c in range(3):
                dst[c, i] = u[c] + w3[i] * rest[c]

    def two(t, carry):
        coarse(u3a, u3b)
        coarse(u3b, u3a)
        return carry

    lax.fori_loop(0, 3, two, 0)
    coarse(u3a, u3b)

    c2 = tuple(co2.at[n] for n in range(5))
    lane8 = lanes_of(8)
    lane4 = lanes_of(4)

    def outer(g, carry):
        peer = d - 1 + g
        inside = jnp.logical_and(peer >= 0, peer < SLAB)
        peer = jnp.clip(peer, 0, SLAB - 1)
        for zz in range(4):
            pick = jnp.logical_and((lane4 & 3) == zz, inside)
            for c in range(3):
                v = spread(jnp.where(pick, received[peer & 1, peer // 2, 22 + 4 * c : 26 + 4 * c], 0.0), lane4, 4)
                u2a[c, 4 * g + zz, 0:4] = jnp.zeros((4, 128), F32)
                u2a[c, 4 * g + zz, 4:6] = v[0:2]
                u2a[c, 4 * g + zz, 14:16] = v[2:4]
        return carry

    lax.fori_loop(0, 3, outer, 0)

    def middle(q2, _):
        for c in range(3):
            u2a[c, q2, 6:14] = u2[c, q2, 6:14]

    loop(2, 10, middle, 4)

    def far(g, carry):
        peer = d - 1 + 2 * g
        inside = jnp.logical_and(peer >= 0, peer < SLAB)
        peer = jnp.clip(peer, 0, SLAB - 1)
        for c in range(3):
            v = received[peer & 1, peer // 2, 34 + 4 * c : 38 + 4 * c]
            for f in range(2):
                for half in range(2):
                    pick = jnp.logical_and((lane4 & 3) == 2 * half + f, inside)
                    u2a[c, 10 * g + f, 6 + 4 * half : 10 + 4 * half] = spread(jnp.where(pick, v, 0.0), lane4, 4)
        return carry

    lax.fori_loop(0, 2, far, 0)

    def add_coarse(t, s):
        z = 2 * d - 2 + t
        i = (z + 32) & 3
        j = z >> 2
        for c in range(3):
            v = jnp.where((lane8 & 7) == j, u3b[c, i, 8:16], 0.0)
            double_rows(spread(v, lane8, 8), tmp.at[3 * s + c])
            for q2 in (2 * t, 2 * t + 1):
                u2a[c, q2, 4:16] = u2a[c, q2, 4:16] + tmp[3 * s + c, 0:12]

    loop(0, 6, add_coarse, 3)
    sweep((1, 11), b2, u2a, u2b, k2, c2, 4)
    sweep((2, 10), b2, u2b, u2a, k2, c2, 4)

    c1 = tuple(co1.at[n] for n in range(5))

    def fill(p):
        for ref, v in zip(c1, coefficients(k1[p], None, k1[p + 1], 0.25, 2, None, t1[p])):
            ref[p] = v

    each((0, 15), fill)

    def add_middle(q2, s):
        for c in range(3):
            double_rows(u2a[c, q2, 6:14], tmp.at[3 * s + c])
            more = tmp[3 * s + c, 0:16]
            for p in (2 * q2 - 4, 2 * q2 - 3):
                u1a[c, p] = u1[c, p] + more

    loop(2, 10, add_middle, 4)
    sweep((1, 15), b1, u1a, u1b, k1, c1, 2)
    sweep((2, 14), b1, u1b, u1a, k1, c1, 2)

    c0 = tuple(co0.at[n] for n in range(5))
    def add_fine(p1, s):
        for c in range(3):
            double_rows(u1a[c, p1], tmp.at[3 * s + c])
            more = tmp[3 * s + c, 4:28]
            for p in (2 * p1 - 3, 2 * p1 - 2):
                u0a[c, p] = u0[c, p] + m0[p] * more

    loop(2, 14, add_fine, 4)
    sweep((3, 23), b0, u0a, u0b, k0, c0, 1, FINE)
    sweep((4, 22), b0, u0b, u0a, k0, c0, 1, FINE)

    def last(z):
        p = z + 5
        u, rest = left_over(p, b0, u0a, k0, c0, 1, FINE)
        for c in range(3):
            field[c, z] = u[c][4:20]
            residual[c, z] = (m0[p] * rest[c])[4:20]

    each((0, 16), last)


def struct(*shape):
    return jax.ShapeDtypeStruct(shape, F32)


def call(kernel, name, outs, scratch, *args, smem=0, alias=None, flops=0):
    vmem = pl.BlockSpec(memory_space=pltpu.VMEM)
    specs = [pl.BlockSpec(memory_space=pltpu.SMEM)] * smem
    return pl.pallas_call(
        kernel,
        name=name,
        out_shape=outs,
        in_specs=specs + [vmem] * (len(args) - len(specs)),
        out_specs=jax.tree.map(lambda _: vmem, outs),
        scratch_shapes=[pltpu.VMEM(s, F32) for s in scratch],
        input_output_aliases=alias or {},
        cost_estimate=pl.CostEstimate(flops=flops, bytes_accessed=flops, transcendentals=0) if flops else None,
        compiler_params=pltpu.CompilerParams(vmem_limit_bytes=40 * 1024 * 1024),
    )(*args)


def shift(block, axis, count, by):
    pairs = [(i, i + by) for i in range(count) if 0 <= i + by < count]
    return lax.ppermute(block, axis, pairs)


def slab_neighbours(to_partner, to_cross):
    pairs = []
    for i in range(1, SLAB - 1, 2):
        pairs += [(i, i + 1), (i + 1, i)]
    cross = lax.ppermute(to_cross, "slab", pairs)
    groups = [[i, i + 1] for i in range(0, SLAB, 2)]
    return lax.all_gather(to_partner, "slab", axis_index_groups=groups), cross


def on_device(load, density, moduli, fixed):
    place = jnp.stack([lax.axis_index("slab"), lax.axis_index("col")]).astype(jnp.int32)
    own = struct(16, 16, 128)
    raw = jnp.concatenate([load, density[None].astype(F32), fixed[None].astype(F32)], axis=0)
    k, m, low, high = call(
        prep_kernel, "prep", (own, own, struct(16, 24, 128), struct(16, 24, 128)), [], moduli, raw, smem=1
    )
    y_low = shift(high, "col", COL, 1)
    y_high = shift(low, "col", COL, -1)
    to_partner, to_cross = call(
        planes_kernel, "planes", (struct(544, 128), struct(544, 128)), [],
        place, raw, k, m, y_low, y_high, smem=1,
    )
    partner, cross = slab_neighbours(to_partner, to_cross)
    part0, full0, full0v = (26, 24, 128), (26, 32, 128), (3, 26, 24, 128)
    kept = (struct(*full0v), struct(*full0v), struct(*full0), struct(*part0), struct(20, 8, 128),
            struct(5, *part0), struct(*full0v), struct(10, 16, 128), struct(8, 8, 128))
    rows = [(16, 48, 128)]
    near = call(
        fine_near_kernel, "fine_near", kept, rows, place, raw, k, m, y_low, y_high, partner,
        smem=1, flops=8_000_000,
    )
    b0, u0, k0, m0, message, co0, *_ = call(
        fine_far_kernel, "fine_far", kept, rows, place, cross, *near,
        smem=1, alias={2 + n: n for n in range(len(kept))},
    )
    y_low = shift(message, "col", COL, 1)
    y_high = shift(message, "col", COL, -1)
    wide = jnp.concatenate([y_low, message, y_high], axis=1)
    partner, cross = slab_neighbours(wide, wide)
    full1, full1v, more1 = (24, 24, 128), (3, 24, 24, 128), (25, 24, 128)
    part1, part1v = (16, 16, 128), (3, 16, 16, 128)
    full2, full2v = (12, 16, 128), (3, 12, 16, 128)
    kept = (struct(*full1v), struct(*full1v), struct(*more1), struct(*full1), struct(5, *full1), struct(*full1v),
            struct(*full2v), struct(*full2))
    near = call(
        middle_near_kernel, "middle_near", kept, rows, place, wide, partner, smem=1, flops=8_000_000
    )
    outs = call(
        middle_far_kernel, "middle_far",
        kept + (struct(*part1v), struct(*part1v), struct(*part1), struct(*part1), struct(*full2v),
                struct(COL, 8, 128), struct(5, *full2)),
        [full2v] + rows, place, cross, *near,
        smem=1, alias={2 + n: n for n in range(len(kept))},
    )
    b2, k2, b1, u1, k1, t1, u2, packed, co2 = outs[6:]
    received = lax.all_to_all(packed, "col", 0, 0)
    window = call(window_kernel, "window", struct(SLAB // 2, 48, 128), [(48, 128)], place, received, u2, smem=1)
    groups = [list(range(par, SLAB, 2)) for par in range(2)]
    received = lax.all_to_all(window, "slab", 0, 0, axis_index_groups=groups)
    received = lax.all_gather(received, "slab", axis_index_groups=[[i, i + 1] for i in range(0, SLAB, 2)])
    full3, full3v = (4, 24, 128), (3, 4, 24, 128)
    return call(
        upper_kernel, "upper",
        (struct(3, 16, 16, 128), struct(3, 16, 16, 128)),
        [full3v, full3, (5,) + full3, full3v, full3v, full2v, full2v,
         (5,) + part1, part1v, part1v, full0v, full0v, (16, 48, 128)],
        place, received, u2, b2, k2, co2, b1, u1, k1, t1, b0, u0, k0, m0, co0, smem=1,
    )


def solution(mesh):
    placed = (P(None, "slab", "col", None), P("slab", "col", None), P(), P("slab", "col", None))
    return jax.shard_map(
        on_device,
        mesh=mesh,
        in_specs=placed,
        out_specs=(P(None, "slab", "col", None), P(None, "slab", "col", None)),
        check_vma=False,
    )
```

```python
import jax
import jax.numpy as jnp
from jax import lax
from jax.experimental import pallas as pl
from jax.experimental.pallas import tpu as pltpu
from jax.sharding import PartitionSpec as P

CLASSES = 8
OMEGA = 0.6
COUPLE = 0.05
SLAB = 16
COL = 32
F32 = jnp.float32


def loop(low, high, body, unroll):
    def step(t, carry):
        for q in range(unroll):
            body(low + t * unroll + q, q)
        return carry

    assert (high - low) % unroll == 0
    lax.fori_loop(0, (high - low) // unroll, step, 0)


def span(low, count, body, unroll=None):
    fits = [n for n in (8, 7, 6, 5, 4, 11, 3, 2) if count % n == 0]
    loop(0, count, lambda n, q: body(low + n, q), unroll or fits[0])


def each(planes, body):
    count = planes[2] if len(planes) == 3 else planes[1] - planes[0]
    span(planes[0], count, lambda p, q: body(p))


def lanes_of(rows):
    return lax.broadcasted_iota(jnp.int32, (rows, 128), 1)


def lane_next(v, step):
    return pltpu.roll(v, 128 - step, 1)


def lane_prev(v, step):
    return pltpu.roll(v, step, 1)


def row_next(v):
    return pltpu.roll(v, v.shape[0] - 1, 0)


def row_prev(v):
    return pltpu.roll(v, 1, 0)


def spread(v, lane, width):
    step = 1
    while step < width:
        v = v + jnp.where((lane & step) != 0, lane_prev(v, step), lane_next(v, step))
        step *= 2
    return v


def coefficients(k, k_lo, k_hi, scale, step, mask, total=None):
    lane = lanes_of(k.shape[0])
    half = 0.5 * scale
    k_next = lane_next(k, step)
    cx = jnp.where(lane < 128 - step, half * (k + k_next), 0.0)
    ky = row_next(k)
    cy = half * (k + ky)
    cz = half * (k + k_hi)
    if total is None:
        sides = jnp.where(lane < 128 - step, k_next, 0.0) + jnp.where(lane >= step, lane_prev(k, step), 0.0)
        total = half * (6.0 * k + sides + ky + row_prev(k) + k_lo + k_hi)
    diag = total + 2.0 * COUPLE * k
    top = OMEGA if mask is None else OMEGA * mask
    weight = jnp.where(k > 0.0, top / diag, 0.0)
    return cx, cy, cz, total + COUPLE * k, weight


def remainder(b, u, u_lo, u_hi, k, cx, cy, cz, cz_lo, e, step):
    cx_lo = lane_prev(cx, step)
    cy_lo = row_prev(cy)
    shared = COUPLE * k * (u[0] + u[1] + u[2])
    out = []
    for c in range(3):
        v = u[c]
        around = cx * lane_next(v, step) + cx_lo * lane_prev(v, step)
        around = around + cy * row_next(v) + cy_lo * row_prev(v)
        around = around + cz * u_hi[c] + cz_lo * u_lo[c]
        out.append((b[c] - shared) + (around - e * v))
    return out


def fill_coefficients(k_ref, co, planes, scale, step, total_ref=None):
    def body(p):
        total = None if total_ref is None else total_ref[p]
        values = coefficients(k_ref[p], k_ref[p - 1], k_ref[p + 1], scale, step, None, total)
        for ref, v in zip(co, values):
            ref[p] = v

    each(planes, body)


def fine_coefficients(k_ref, m_ref, co, planes):
    def body(p):
        k = k_ref[p, 4:28]
        k_lo, k_hi = k_ref[p - 1, 4:28], k_ref[p + 1, 4:28]
        ky, ky_lo = k_ref[p, 5:29], k_ref[p, 3:27]
        lane = lanes_of(24)
        k_next = jnp.where(lane < 127, lane_next(k, 1), 0.0)
        k_prev = jnp.where(lane >= 1, lane_prev(k, 1), 0.0)
        total = 0.5 * (6.0 * k + k_next + k_prev + ky + ky_lo + k_lo + k_hi)
        values = (
            jnp.where(lane < 127, 0.5 * (k + k_next), 0.0), 0.5 * (k + ky), 0.5 * (k + k_hi),
            total + COUPLE * k,
            jnp.where(k > 0.0, OMEGA * m_ref[p] / (total + 2.0 * COUPLE * k), 0.0),
        )
        for ref, v in zip(co, values):
            ref[p] = v

    each(planes, body)


def left_over(p, b_ref, u_ref, k_ref, co, step, rows=slice(None)):
    cx_ref, cy_ref, cz_ref, e_ref, _ = co
    b = [b_ref[c, p] for c in range(3)]
    u = [u_ref[c, p] for c in range(3)]
    lo = [u_ref[c, p - 1] for c in range(3)]
    hi = [u_ref[c, p + 1] for c in range(3)]
    k = k_ref[p, rows]
    return u, remainder(b, u, lo, hi, k, cx_ref[p], cy_ref[p], cz_ref[p], cz_ref[p - 1], e_ref[p], step)


def sweep(planes, b_ref, u_ref, new_ref, k_ref, co, step, rows=slice(None)):
    def body(p):
        u, rest = left_over(p, b_ref, u_ref, k_ref, co, step, rows)
        w = co[4][p]
        for c in range(3):
            new_ref[c, p] = u[c] + w * rest[c]

    each(planes, body)


def first_sweep(planes, b_ref, new_ref, w_ref):
    def body(p):
        w = w_ref[p]
        for c in range(3):
            new_ref[c, p] = w * b_ref[c, p]

    each(planes, body)


def block_mean(a, b, tmp, step):
    lane = lanes_of(a.shape[0])
    s = a + b
    s = s + jnp.where((lane & step) != 0, lane_prev(s, step), lane_next(s, step))
    n = a.shape[0]
    tmp[0:n] = s
    return 0.125 * (tmp[pl.ds(0, n // 2, stride=2)] + tmp[pl.ds(1, n // 2, stride=2)])


def double_rows(v, tmp):
    n = v.shape[0]
    tmp[pl.ds(0, n, stride=2)] = v
    tmp[pl.ds(1, n, stride=2)] = v


FINE = slice(4, 28)


def prep_kernel(moduli, raw, k_out, m_out, low, high):
    def body(z):
        d = raw[3, z]
        k = jnp.zeros((16, 128), F32)
        for klass in range(CLASSES):
            k = jnp.where(d == float(klass), moduli[klass], k)
        m = 1.0 - raw[4, z]
        k_out[z] = k
        m_out[z] = m
        for c in range(3):
            low[z, 4 * c : 4 * c + 4] = raw[c, z, 0:4]
            high[z, 4 * c : 4 * c + 4] = raw[c, z, 12:16]
        low[z, 12:16] = m[0:4]
        high[z, 12:16] = m[12:16]
        low[z, 16:24] = k[0:8]
        high[z, 16:24] = k[8:16]

    each((0, 16), body)


def planes_kernel(place, load, k, m, from_low, from_high, partner, cross):
    odd = place[0] & 1
    for out, start, k_start in (
        (partner, 12 * (1 - odd), 11 * (1 - odd)), (cross, 12 * odd, 11 * odd),
    ):
        for q in range(4):
            z = start + q
            for a in range(4):
                base = 24 * (4 * a + q)
                own = load[a, z] if a < 3 else m[z]
                out[base : base + 4] = from_low[z, 4 * a : 4 * a + 4]
                out[base + 4 : base + 20] = own
                out[base + 20 : base + 24] = from_high[z, 4 * a : 4 * a + 4]
        for q in range(5):
            z = k_start + q
            base = 384 + 32 * q
            out[base : base + 8] = from_low[z, 16:24]
            out[base + 8 : base + 24] = k[z]
            out[base + 24 : base + 32] = from_high[z, 16:24]


def fine_part(odd, near, b, u, k, m, message, co_out, first, k1, sums, tmp):
    co = tuple(co_out.at[n] for n in range(5))
    even = 1 - odd
    if near:
        (c_low, c_count), (s_low, s_count) = (1 + 6 * even, 18), (2 + 6 * even, 16)
        (k_low, k_count), (d_low, d_count) = (2 * even, 8), (2 * even, 6)
    else:
        (c_low, c_count), (s_low, s_count) = (1 + 18 * odd, 6), (2 + 16 * odd, 6)
        (k_low, k_count), (d_low, d_count) = (8 * odd, 2), (6 * odd, 2)
    fine_coefficients(k, m, co, (c_low, None, c_count))
    first_sweep((c_low, None, c_count), b, first, co[4])
    sweep((s_low, None, s_count), b, first, u, k, co, 1, FINE)

    def coarse_k(n, q):
        p = 2 * n + 3
        k1[n] = block_mean(k[p], k[p + 1], tmp.at[q], 1)

    span(k_low, k_count, coarse_k)
    lane = lanes_of(8)
    odd_lane = (lane & 1) != 0
    lane = lanes_of(16)

    def down(z1, s):
        p = 2 * z1 + 5
        rests = [left_over(q, b, u, k, co, 1, FINE)[1] for q in (p, p + 1)]
        parts = [
            block_mean(m[p] * rests[0][c], m[p + 1] * rests[1][c], tmp.at[3 * s + c], 1)[2:10] for c in range(3)
        ]
        centre = k1[z1 + 1]
        sides = jnp.where(lane < 126, lane_next(centre, 2), 0.0) + jnp.where(lane >= 2, lane_prev(centre, 2), 0.0)
        total = 0.125 * (6.0 * centre + sides + row_next(centre) + row_prev(centre) + k1[z1] + k1[z1 + 2])
        message[z1] = jnp.where(odd_lane, parts[1], parts[0])
        message[8 + z1] = jnp.where(odd_lane, centre[4:12], parts[2])
        sums[z1] = total[4:12]

    span(d_low, d_count, down, 3 if near else 2)


def place_planes(src, high, b, m, k):
    start, k_start = 1 + 20 * high, 21 * high
    for q in range(4):
        for a in range(4):
            part = src[24 * (4 * a + q) : 24 * (4 * a + q) + 24]
            if a < 3:
                b[a, start + q] = part
            else:
                m[start + q] = part
    for q in range(5):
        k[k_start + q] = src[384 + 32 * q : 416 + 32 * q]


def fine_near_kernel(place, load, k_own, m_own, y_low, y_high, partner, *refs):
    b, u, k, m, message, co_out, first, k1, sums, tmp = refs
    odd = place[0] & 1

    def own(z):
        p = z + 5
        for c in range(3):
            b[c, p, 0:4] = y_low[z, 4 * c : 4 * c + 4]
            b[c, p, 4:20] = load[c, z]
            b[c, p, 20:24] = y_high[z, 4 * c : 4 * c + 4]
        m[p, 0:4] = y_low[z, 12:16]
        m[p, 4:20] = m_own[z]
        m[p, 20:24] = y_high[z, 12:16]
        k[p, 0:8] = y_low[z, 16:24]
        k[p, 8:24] = k_own[z]
        k[p, 24:32] = y_high[z, 16:24]

    each((0, 16), own)
    place_planes(partner.at[1 - odd], 1 - odd, b, m, k)
    fine_part(odd, True, *refs)


def fine_far_kernel(place, cross, *refs):
    refs = refs[9:]
    b, u, k, m, message, co_out, first, k1, sums, tmp = refs
    odd = place[0] & 1
    place_planes(cross, odd, b, m, k)
    fine_part(odd, False, *refs)
    odd_lane = (lanes_of(8) & 1) != 0
    for z1 in range(4):
        message[16 + z1] = jnp.where(odd_lane, sums[z1 + 4], sums[z1])


def middle_part(odd, near, b1, u1, k1, t1, co_out, first, b2, k2, tmp):
    co = tuple(co_out.at[n] for n in range(5))
    even = 1 - odd
    if near:
        (c_low, c_count), (s_low, s_count) = (8 * even, 16), (1 + 8 * even, 14)
        (k_low, k_count), (d_low, d_count) = (4 * even, 8), (1 + 4 * even, 6)
    else:
        (c_low, c_count), (s_low, s_count) = (15 * odd, 9), (1 + 14 * odd, 8)
        (k_low, k_count), (d_low, d_count) = (8 * odd, 4), (1 + 6 * odd, 4)

    def fill(p):
        for ref, v in zip(co, coefficients(k1[p], None, k1[p + 1], 0.25, 2, None, t1[p])):
            ref[p] = v
        for c in range(3):
            first[c, p] = co[4][p] * b1[c, p]

    each((c_low, None, c_count), fill)
    sweep((s_low, None, s_count), b1, first, u1, k1, co, 2)

    def coarse_k(q2, s):
        k2[q2, 4:16] = block_mean(k1[2 * q2], k1[2 * q2 + 1], tmp.at[s], 2)
        k2[q2, 0:4] = jnp.zeros((4, 128), F32)

    span(k_low, k_count, coarse_k, 4)

    def down(q2, s):
        rests = [left_over(p, b1, u1, k1, co, 2)[1] for p in (2 * q2, 2 * q2 + 1)]
        for c in range(3):
            b2[c, q2, 4:16] = block_mean(rests[0][c], rests[1][c], tmp.at[3 * s + c], 2)
            b2[c, q2, 0:4] = jnp.zeros((4, 128), F32)

    span(d_low, d_count, down, 3 if near else 4)


def take(src, start, b1, k1, t1):
    odd_lane = (lanes_of(24) & 1) != 0
    for q in range(8):
        p = start + q
        v = src[q]
        b1[0, p] = jnp.where(odd_lane, lane_prev(v, 1), v)
        b1[1, p] = jnp.where(odd_lane, v, lane_next(v, 1))
        v = src[8 + q]
        b1[2, p] = jnp.where(odd_lane, lane_prev(v, 1), v)
        k1[p] = jnp.where(odd_lane, v, lane_next(v, 1))
    for q in range(4):
        v = src[16 + q]
        t1[start + q] = jnp.where(odd_lane, lane_prev(v, 1), v)
        t1[start + 4 + q] = jnp.where(odd_lane, v, lane_next(v, 1))


def middle_near_kernel(place, own, partner, *refs):
    b1, u1, k1, t1 = refs[:4]
    odd = place[0] & 1
    take(own, 8, b1, k1, t1)
    take(partner.at[1 - odd], 16 * (1 - odd), b1, k1, t1)
    k1[24] = jnp.zeros((24, 128), F32)
    middle_part(odd, True, *refs)


def middle_far_kernel(place, cross, *refs):
    refs = refs[8:]
    b1, u1, k1, t1, co_out, first, b2, k2 = refs[:8]
    b1_out, u1_out, k1_out, t1_out, u2b, packed, co2_out, u2a, tmp = refs[8:]
    odd = place[0] & 1
    take(cross, 16 * odd, b1, k1, t1)
    middle_part(odd, False, b1, u1, k1, t1, co_out, first, b2, k2, tmp)

    def keep(p):
        k1_out[p] = k1[p + 4, 4:20]
        t1_out[p] = t1[p + 4, 4:20]
        for c in range(3):
            b1_out[c, p] = b1[c, p + 4, 4:20]
            u1_out[c, p] = u1[c, p + 4, 4:20]

    each((0, 16), keep)
    co2 = tuple(co2_out.at[n] for n in range(5))
    fill_coefficients(k2, co2, (1, 11), 0.0625, 4)
    co2[2][0] = (0.5 * 0.0625) * (k2[0] + k2[1])
    first_sweep((1, 11), b2, u2a, co2[4])
    sweep((2, 10), b2, u2a, u2b, k2, co2, 4)
    j = place[0] // 2
    lane = lanes_of(8)
    group = lane & 7
    pack = jnp.zeros((8, 128), F32)
    for zz in range(2):
        rests = [left_over(p, b2, u2b, k2, co2, 4)[1] for p in (4 + 2 * zz, 5 + 2 * zz)]
        parts = [block_mean(rests[0][c], rests[1][c], tmp.at[4 * zz + c], 4) for c in range(3)]
        parts.append(block_mean(k2[4 + 2 * zz], k2[5 + 2 * zz], tmp.at[4 * zz + 3], 4))
        for a in range(4):
            pack = jnp.where(group == ((j + 2 * a + zz) & 7), parts[a], pack)
    quad = lane & 3
    low, high = tmp.at[8], tmp.at[9]
    low[0:2] = pack[4:6]
    high[0:2] = pack[4:6]
    for c in range(3):
        v = u2b[c, 7, 8:16]
        for zz in (2, 1, 0):
            v = jnp.where(quad == zz, u2b[c, 4 + zz, 8:16], v)
        low[2 + 2 * c : 4 + 2 * c] = v[2:4]
        high[2 + 2 * c : 4 + 2 * c] = v[0:2]
    to_low, to_high = low[0:8], high[0:8]
    for peer in range(COL):
        packed[peer] = jnp.where(place[1] < peer, to_high, to_low)


def window_kernel(place, received, u2, out, tmp):
    c, d = place[1], place[0]
    for q in range(11):
        peer = c - 5 + q
        inside = jnp.logical_and(peer >= 0, peer < COL).astype(F32)
        tmp[2 * q : 2 * q + 2] = inside * received[jnp.clip(peer, 0, COL - 1), 0:2]
    for comp in range(3):
        for q, peer in ((0, c - 1), (1, c + 1)):
            inside = jnp.logical_and(peer >= 0, peer < COL).astype(F32)
            part = received[jnp.clip(peer, 0, COL - 1), 2 + 2 * comp : 4 + 2 * comp]
            base = 24 + 4 * comp + 2 * q
            tmp[base : base + 2] = inside * part
    quad = lanes_of(4) & 3
    tmp[22:24] = jnp.zeros((2, 128), F32)

    def inner(near):
        for comp in range(3):
            a = [u2[comp, 4 + near + f, 6:10] for f in range(2)]
            b = [u2[comp, 4 + near + f, 10:14] for f in range(2)]
            v = jnp.where(quad == 0, a[0], jnp.where(quad == 1, a[1], jnp.where(quad == 2, b[0], b[1])))
            tmp[36 + 4 * comp : 40 + 4 * comp] = v
        return tmp[...]

    to_high = inner(0)
    to_low = inner(2)
    for q in range(SLAB // 2):
        out[q] = jnp.where(q + 1 - (d & 1) > d // 2, to_high, to_low)


def upper_kernel(place, received, u2, b2, k2, co2, b1, u1, k1, t1, b0, u0, k0, m0, co0,
                 field, residual,
                 b3, k3, co3, u3a, u3b, u2a, u2b, co1, u1a, u1b, u0a, u0b, tmp):
    d = place[0]
    lane = lanes_of(24)
    group = lane & 7

    def unpack(a, carry):
        mixes = [jnp.zeros((24, 128), F32)] * 8
        for j in range(8):
            v = received[a, j, 0:24]
            for r in range(8):
                mixes[r] = jnp.where(group == ((j + r) & 7), v, mixes[r])
        for r in range(8):
            mix = mixes[r]
            if r:
                mix = jnp.where(group < 8 - r, lane_next(mix, r), lane_prev(mix, 8 - r))
            arr, plane = r // 2, 2 * a + r % 2
            if arr < 3:
                b3[arr, plane] = mix
            else:
                k3[plane] = mix
        return carry

    lax.fori_loop(0, 2, unpack, 0)

    def above(v_of, i):
        return v_of(i + 1) if i < 3 else jnp.where(group < 7, lane_next(v_of(0), 1), 0.0)

    def below(v_of, i):
        return v_of(i - 1) if i > 0 else jnp.where(group > 0, lane_prev(v_of(3), 1), 0.0)

    cx3, cy3, cz3, e3, w3 = (co3.at[n] for n in range(5))
    for i in range(4):
        cx, cy, cz, e, w = coefficients(
            k3[i], below(lambda q: k3[q], i), above(lambda q: k3[q], i), 1.0 / 64.0, 8, None
        )
        cx3[i] = cx
        cy3[i] = cy
        cz3[i] = cz
        e3[i] = e
        w3[i] = w
        for c in range(3):
            u3a[c, i] = w * b3[c, i]

    def coarse(src, dst):
        for i in range(4):
            u = [src[c, i] for c in range(3)]
            lo = [below(lambda q: src[c, q], i) for c in range(3)]
            hi = [above(lambda q: src[c, q], i) for c in range(3)]
            b = [b3[c, i] for c in range(3)]
            cz_lo = below(lambda q: cz3[q], i)
            rest = remainder(b, u, lo, hi, k3[i], cx3[i], cy3[i], cz3[i], cz_lo, e3[i], 8)
            for c in range(3):
                dst[c, i] = u[c] + w3[i] * rest[c]

    def two(t, carry):
        coarse(u3a, u3b)
        coarse(u3b, u3a)
        return carry

    lax.fori_loop(0, 3, two, 0)
    coarse(u3a, u3b)

    c2 = tuple(co2.at[n] for n in range(5))
    lane8 = lanes_of(8)
    lane12 = lanes_of(12)

    def outer(g, carry):
        peer = d - 1 + g
        inside = jnp.logical_and(peer >= 0, peer < SLAB)
        peer = jnp.clip(peer, 0, SLAB - 1)
        rows = received[peer & 1, peer // 2, 24:36]
        for zz in range(4):
            pick = jnp.logical_and((lane12 & 3) == zz, inside)
            v = spread(jnp.where(pick, rows, 0.0), lane12, 4)
            for c in range(3):
                u2a[c, 4 * g + zz, 0:4] = jnp.zeros((4, 128), F32)
                u2a[c, 4 * g + zz, 4:6] = v[4 * c : 4 * c + 2]
                u2a[c, 4 * g + zz, 14:16] = v[4 * c + 2 : 4 * c + 4]
        return carry

    lax.fori_loop(0, 3, outer, 0)

    def middle(q2, _):
        for c in range(3):
            u2a[c, q2, 6:14] = u2[c, q2, 6:14]

    loop(2, 10, middle, 4)

    def far(g, carry):
        peer = d - 1 + 2 * g
        inside = jnp.logical_and(peer >= 0, peer < SLAB)
        peer = jnp.clip(peer, 0, SLAB - 1)
        rows = received[peer & 1, peer // 2, 36:48]
        for f in range(2):
            for half in range(2):
                pick = jnp.logical_and((lane12 & 3) == 2 * half + f, inside)
                v = spread(jnp.where(pick, rows, 0.0), lane12, 4)
                for c in range(3):
                    u2a[c, 10 * g + f, 6 + 4 * half : 10 + 4 * half] = v[4 * c : 4 * c + 4]
        return carry

    lax.fori_loop(0, 2, far, 0)

    def add_coarse(t, s):
        z = 2 * d - 2 + t
        i = (z + 32) & 3
        j = z >> 2
        for c in range(3):
            v = jnp.where((lane8 & 7) == j, u3b[c, i, 8:16], 0.0)
            double_rows(spread(v, lane8, 8), tmp.at[3 * s + c])
            for q2 in (2 * t, 2 * t + 1):
                u2a[c, q2, 4:16] = u2a[c, q2, 4:16] + tmp[3 * s + c, 0:12]

    loop(0, 6, add_coarse, 3)
    sweep((1, 11), b2, u2a, u2b, k2, c2, 4)
    sweep((2, 10), b2, u2b, u2a, k2, c2, 4)

    c1 = tuple(co1.at[n] for n in range(5))

    def fill(p):
        for ref, v in zip(c1, coefficients(k1[p], None, k1[p + 1], 0.25, 2, None, t1[p])):
            ref[p] = v

    each((0, 15), fill)

    def add_middle(q2, s):
        for c in range(3):
            double_rows(u2a[c, q2, 6:14], tmp.at[3 * s + c])
            more = tmp[3 * s + c, 0:16]
            for p in (2 * q2 - 4, 2 * q2 - 3):
                u1a[c, p] = u1[c, p] + more

    loop(2, 10, add_middle, 4)
    sweep((1, 15), b1, u1a, u1b, k1, c1, 2)
    sweep((2, 14), b1, u1b, u1a, k1, c1, 2)

    c0 = tuple(co0.at[n] for n in range(5))
    def add_fine(p1, s):
        for c in range(3):
            double_rows(u1a[c, p1], tmp.at[3 * s + c])
            more = tmp[3 * s + c, 4:28]
            for p in (2 * p1 - 3, 2 * p1 - 2):
                u0a[c, p] = u0[c, p] + m0[p] * more

    loop(2, 14, add_fine, 4)
    sweep((3, 23), b0, u0a, u0b, k0, c0, 1, FINE)
    sweep((4, 22), b0, u0b, u0a, k0, c0, 1, FINE)

    def last(z):
        p = z + 5
        u, rest = left_over(p, b0, u0a, k0, c0, 1, FINE)
        for c in range(3):
            field[c, z] = u[c][4:20]
            residual[c, z] = (m0[p] * rest[c])[4:20]

    each((0, 16), last)


def struct(*shape):
    return jax.ShapeDtypeStruct(shape, F32)


def call(kernel, name, outs, scratch, *args, smem=0, alias=None, flops=0):
    vmem = pl.BlockSpec(memory_space=pltpu.VMEM)
    specs = [pl.BlockSpec(memory_space=pltpu.SMEM)] * smem
    return pl.pallas_call(
        kernel,
        name=name,
        out_shape=outs,
        in_specs=specs + [vmem] * (len(args) - len(specs)),
        out_specs=jax.tree.map(lambda _: vmem, outs),
        scratch_shapes=[pltpu.VMEM(s, F32) for s in scratch],
        input_output_aliases=alias or {},
        cost_estimate=pl.CostEstimate(flops=flops, bytes_accessed=flops, transcendentals=0) if flops else None,
        compiler_params=pltpu.CompilerParams(vmem_limit_bytes=40 * 1024 * 1024),
    )(*args)


def shift(block, axis, count, by):
    pairs = [(i, i + by) for i in range(count) if 0 <= i + by < count]
    return lax.ppermute(block, axis, pairs)


def slab_neighbours(to_partner, to_cross):
    pairs = []
    for i in range(1, SLAB - 1, 2):
        pairs += [(i, i + 1), (i + 1, i)]
    cross = lax.ppermute(to_cross, "slab", pairs)
    groups = [[i, i + 1] for i in range(0, SLAB, 2)]
    return lax.all_gather(to_partner, "slab", axis_index_groups=groups), cross


def on_device(load, density, moduli, fixed):
    place = jnp.stack([lax.axis_index("slab"), lax.axis_index("col")]).astype(jnp.int32)
    own = struct(16, 16, 128)
    raw = jnp.concatenate([load, density[None].astype(F32), fixed[None].astype(F32)], axis=0)
    k, m, low, high = call(
        prep_kernel, "prep", (own, own, struct(16, 24, 128), struct(16, 24, 128)), [], moduli, raw, smem=1
    )
    y_low = shift(high, "col", COL, 1)
    y_high = shift(low, "col", COL, -1)
    to_partner, to_cross = call(
        planes_kernel, "planes", (struct(544, 128), struct(544, 128)), [],
        place, raw, k, m, y_low, y_high, smem=1,
    )
    partner, cross = slab_neighbours(to_partner, to_cross)
    part0, full0, full0v = (26, 24, 128), (26, 32, 128), (3, 26, 24, 128)
    kept = (struct(*full0v), struct(*full0v), struct(*full0), struct(*part0), struct(20, 8, 128),
            struct(5, *part0), struct(*full0v), struct(10, 16, 128), struct(8, 8, 128))
    rows = [(16, 48, 128)]
    near = call(
        fine_near_kernel, "fine_near", kept, rows, place, raw, k, m, y_low, y_high, partner,
        smem=1, flops=8_000_000,
    )
    b0, u0, k0, m0, message, co0, *_ = call(
        fine_far_kernel, "fine_far", kept, rows, place, cross, *near,
        smem=1, alias={2 + n: n for n in range(len(kept))},
    )
    y_low = shift(message, "col", COL, 1)
    y_high = shift(message, "col", COL, -1)
    wide = jnp.concatenate([y_low, message, y_high], axis=1)
    partner, cross = slab_neighbours(wide, wide)
    full1, full1v, more1 = (24, 24, 128), (3, 24, 24, 128), (25, 24, 128)
    part1, part1v = (16, 16, 128), (3, 16, 16, 128)
    full2, full2v = (12, 16, 128), (3, 12, 16, 128)
    kept = (struct(*full1v), struct(*full1v), struct(*more1), struct(*full1), struct(5, *full1), struct(*full1v),
            struct(*full2v), struct(*full2))
    near = call(
        middle_near_kernel, "middle_near", kept, rows, place, wide, partner, smem=1, flops=8_000_000
    )
    outs = call(
        middle_far_kernel, "middle_far",
        kept + (struct(*part1v), struct(*part1v), struct(*part1), struct(*part1), struct(*full2v),
                struct(COL, 8, 128), struct(5, *full2)),
        [full2v] + rows, place, cross, *near,
        smem=1, alias={2 + n: n for n in range(len(kept))},
    )
    b2, k2, b1, u1, k1, t1, u2, packed, co2 = outs[6:]
    received = lax.all_to_all(packed, "col", 0, 0)
    window = call(window_kernel, "window", struct(SLAB // 2, 48, 128), [(48, 128)], place, received, u2, smem=1)
    groups = [list(range(par, SLAB, 2)) for par in range(2)]
    received = lax.all_to_all(window, "slab", 0, 0, axis_index_groups=groups)
    received = lax.all_gather(received, "slab", axis_index_groups=[[i, i + 1] for i in range(0, SLAB, 2)])
    full3, full3v = (4, 24, 128), (3, 4, 24, 128)
    return call(
        upper_kernel, "upper",
        (struct(3, 16, 16, 128), struct(3, 16, 16, 128)),
        [full3v, full3, (5,) + full3, full3v, full3v, full2v, full2v,
         (5,) + part1, part1v, part1v, full0v, full0v, (16, 48, 128)],
        place, received, u2, b2, k2, co2, b1, u1, k1, t1, b0, u0, k0, m0, co0, smem=1,
    )


def solution(mesh):
    placed = (P(None, "slab", "col", None), P("slab", "col", None), P(), P("slab", "col", None))
    return jax.shard_map(
        on_device,
        mesh=mesh,
        in_specs=placed,
        out_specs=(P(None, "slab", "col", None), P(None, "slab", "col", None)),
        check_vma=False,
    )
```

```python
import jax
import jax.numpy as jnp
from jax import lax
from jax.experimental import pallas as pl
from jax.experimental.pallas import tpu as pltpu
from jax.sharding import PartitionSpec as P

CLASSES = 8
OMEGA = 0.6
COUPLE = 0.05
SLAB = 16
COL = 32
F32 = jnp.float32


def loop(low, high, body, unroll):
    def step(t, carry):
        for q in range(unroll):
            body(low + t * unroll + q, q)
        return carry

    assert (high - low) % unroll == 0
    lax.fori_loop(0, (high - low) // unroll, step, 0)


def span(low, count, body, unroll=None):
    fits = [n for n in (8, 7, 6, 5, 4, 11, 3, 2) if count % n == 0]
    loop(0, count, lambda n, q: body(low + n, q), unroll or fits[0])


def each(planes, body):
    count = planes[2] if len(planes) == 3 else planes[1] - planes[0]
    span(planes[0], count, lambda p, q: body(p))


def lanes_of(rows):
    return lax.broadcasted_iota(jnp.int32, (rows, 128), 1)


def lane_next(v, step):
    return pltpu.roll(v, 128 - step, 1)


def lane_prev(v, step):
    return pltpu.roll(v, step, 1)


def row_next(v):
    return pltpu.roll(v, v.shape[0] - 1, 0)


def row_prev(v):
    return pltpu.roll(v, 1, 0)


def spread(v, lane, width):
    step = 1
    while step < width:
        v = v + jnp.where((lane & step) != 0, lane_prev(v, step), lane_next(v, step))
        step *= 2
    return v


def coefficients(k, k_lo, k_hi, scale, step, mask, total=None):
    lane = lanes_of(k.shape[0])
    half = 0.5 * scale
    k_next = lane_next(k, step)
    cx = jnp.where(lane < 128 - step, half * (k + k_next), 0.0)
    ky = row_next(k)
    cy = half * (k + ky)
    cz = half * (k + k_hi)
    if total is None:
        sides = jnp.where(lane < 128 - step, k_next, 0.0) + jnp.where(lane >= step, lane_prev(k, step), 0.0)
        total = half * (6.0 * k + sides + ky + row_prev(k) + k_lo + k_hi)
    diag = total + 2.0 * COUPLE * k
    top = OMEGA if mask is None else OMEGA * mask
    weight = jnp.where(k > 0.0, top / diag, 0.0)
    return cx, cy, cz, total + COUPLE * k, weight


def remainder(b, u, u_lo, u_hi, k, cx, cy, cz, cz_lo, e, step):
    cx_lo = lane_prev(cx, step)
    cy_lo = row_prev(cy)
    shared = COUPLE * k * (u[0] + u[1] + u[2])
    out = []
    for c in range(3):
        v = u[c]
        around = cx * lane_next(v, step) + cx_lo * lane_prev(v, step)
        around = around + cy * row_next(v) + cy_lo * row_prev(v)
        around = around + cz * u_hi[c] + cz_lo * u_lo[c]
        out.append((b[c] - shared) + (around - e * v))
    return out


def fill_coefficients(k_ref, co, planes, scale, step, total_ref=None):
    def body(p):
        total = None if total_ref is None else total_ref[p]
        values = coefficients(k_ref[p], k_ref[p - 1], k_ref[p + 1], scale, step, None, total)
        for ref, v in zip(co, values):
            ref[p] = v

    each(planes, body)


def fine_coefficients(k_ref, m_ref, co, planes):
    def body(p):
        k = k_ref[p, 4:28]
        k_lo, k_hi = k_ref[p - 1, 4:28], k_ref[p + 1, 4:28]
        ky, ky_lo = k_ref[p, 5:29], k_ref[p, 3:27]
        lane = lanes_of(24)
        k_next = jnp.where(lane < 127, lane_next(k, 1), 0.0)
        k_prev = jnp.where(lane >= 1, lane_prev(k, 1), 0.0)
        total = 0.5 * (6.0 * k + k_next + k_prev + ky + ky_lo + k_lo + k_hi)
        values = (
            jnp.where(lane < 127, 0.5 * (k + k_next), 0.0), 0.5 * (k + ky), 0.5 * (k + k_hi),
            total + COUPLE * k,
            jnp.where(k > 0.0, OMEGA * m_ref[p] / (total + 2.0 * COUPLE * k), 0.0),
        )
        for ref, v in zip(co, values):
            ref[p] = v

    each(planes, body)


def left_over(p, b_ref, u_ref, k_ref, co, step, rows=slice(None), part=None):
    cx_ref, cy_ref, cz_ref, e_ref, _ = co
    more, side = part or (0, slice(None))
    n = p + more
    b = [b_ref[c, n, side] for c in range(3)]
    u = [u_ref[c, p] for c in range(3)]
    lo = [u_ref[c, p - 1] for c in range(3)]
    hi = [u_ref[c, p + 1] for c in range(3)]
    k = k_ref[n, rows if part is None else side]
    cx, cy, cz, cz_lo, e = cx_ref[n, side], cy_ref[n, side], cz_ref[n, side], cz_ref[n - 1, side], e_ref[n, side]
    return u, remainder(b, u, lo, hi, k, cx, cy, cz, cz_lo, e, step)


def sweep(planes, b_ref, u_ref, new_ref, k_ref, co, step, rows=slice(None), part=None):
    more, side = part or (0, slice(None))

    def body(p):
        u, rest = left_over(p, b_ref, u_ref, k_ref, co, step, rows, part)
        w = co[4][p + more, side]
        for c in range(3):
            new_ref[c, p] = u[c] + w * rest[c]

    each(planes, body)


def first_sweep(planes, b_ref, new_ref, w_ref):
    def body(p):
        w = w_ref[p]
        for c in range(3):
            new_ref[c, p] = w * b_ref[c, p]

    each(planes, body)


def block_mean(a, b, tmp, step):
    lane = lanes_of(a.shape[0])
    s = a + b
    s = s + jnp.where((lane & step) != 0, lane_prev(s, step), lane_next(s, step))
    n = a.shape[0]
    tmp[0:n] = s
    return 0.125 * (tmp[pl.ds(0, n // 2, stride=2)] + tmp[pl.ds(1, n // 2, stride=2)])


def double_rows(v, tmp):
    n = v.shape[0]
    tmp[pl.ds(0, n, stride=2)] = v
    tmp[pl.ds(1, n, stride=2)] = v


FINE = slice(4, 28)


def prep_kernel(moduli, raw, k_out, m_out, low, high):
    def body(z):
        d = raw[3, z]
        k = jnp.zeros((16, 128), F32)
        for klass in range(CLASSES):
            k = jnp.where(d == float(klass), moduli[klass], k)
        m = 1.0 - raw[4, z]
        k_out[z] = k
        m_out[z] = m
        for c in range(3):
            low[z, 4 * c : 4 * c + 4] = raw[c, z, 0:4]
            high[z, 4 * c : 4 * c + 4] = raw[c, z, 12:16]
        low[z, 12:16] = m[0:4]
        high[z, 12:16] = m[12:16]
        low[z, 16:24] = k[0:8]
        high[z, 16:24] = k[8:16]

    each((0, 16), body)


def planes_kernel(place, load, k, m, from_low, from_high, partner, cross):
    odd = place[0] & 1
    for out, start, k_start in (
        (partner, 12 * (1 - odd), 11 * (1 - odd)), (cross, 12 * odd, 11 * odd),
    ):
        for q in range(4):
            z = start + q
            for a in range(4):
                base = 24 * (4 * a + q)
                own = load[a, z] if a < 3 else m[z]
                out[base : base + 4] = from_low[z, 4 * a : 4 * a + 4]
                out[base + 4 : base + 20] = own
                out[base + 20 : base + 24] = from_high[z, 4 * a : 4 * a + 4]
        for q in range(5):
            z = k_start + q
            base = 384 + 32 * q
            out[base : base + 8] = from_low[z, 16:24]
            out[base + 8 : base + 24] = k[z]
            out[base + 24 : base + 32] = from_high[z, 16:24]


def fine_part(odd, near, b, u, k, m, message, co_out, first, k1, sums, tmp):
    co = tuple(co_out.at[n] for n in range(5))
    even = 1 - odd
    if near:
        (c_low, c_count), (s_low, s_count) = (1 + 6 * even, 18), (2 + 6 * even, 16)
        (k_low, k_count), (d_low, d_count) = (2 * even, 8), (2 * even, 6)
    else:
        (c_low, c_count), (s_low, s_count) = (1 + 18 * odd, 6), (2 + 16 * odd, 6)
        (k_low, k_count), (d_low, d_count) = (8 * odd, 2), (6 * odd, 2)
    fine_coefficients(k, m, co, (c_low, None, c_count))
    first_sweep((c_low, None, c_count), b, first, co[4])
    sweep((s_low, None, s_count), b, first, u, k, co, 1, FINE)

    def coarse_k(n, q):
        p = 2 * n + 3
        k1[n] = block_mean(k[p], k[p + 1], tmp.at[q], 1)

    span(k_low, k_count, coarse_k)
    lane = lanes_of(8)
    odd_lane = (lane & 1) != 0
    lane = lanes_of(16)

    def down(z1, s):
        p = 2 * z1 + 5
        rests = [left_over(q, b, u, k, co, 1, FINE)[1] for q in (p, p + 1)]
        parts = [
            block_mean(m[p] * rests[0][c], m[p + 1] * rests[1][c], tmp.at[3 * s + c], 1)[2:10] for c in range(3)
        ]
        centre = k1[z1 + 1]
        sides = jnp.where(lane < 126, lane_next(centre, 2), 0.0) + jnp.where(lane >= 2, lane_prev(centre, 2), 0.0)
        total = 0.125 * (6.0 * centre + sides + row_next(centre) + row_prev(centre) + k1[z1] + k1[z1 + 2])
        message[z1] = jnp.where(odd_lane, parts[1], parts[0])
        message[8 + z1] = jnp.where(odd_lane, centre[4:12], parts[2])
        sums[z1] = total[4:12]

    span(d_low, d_count, down, 3 if near else 2)


def place_planes(src, high, b, m, k):
    start, k_start = 1 + 20 * high, 21 * high
    for q in range(4):
        for a in range(4):
            part = src[24 * (4 * a + q) : 24 * (4 * a + q) + 24]
            if a < 3:
                b[a, start + q] = part
            else:
                m[start + q] = part
    for q in range(5):
        k[k_start + q] = src[384 + 32 * q : 416 + 32 * q]


def fine_near_kernel(place, load, k_own, m_own, y_low, y_high, partner, *refs):
    b, u, k, m, message, co_out, first, k1, sums, tmp = refs
    odd = place[0] & 1

    def own(z):
        p = z + 5
        for c in range(3):
            b[c, p, 0:4] = y_low[z, 4 * c : 4 * c + 4]
            b[c, p, 4:20] = load[c, z]
            b[c, p, 20:24] = y_high[z, 4 * c : 4 * c + 4]
        m[p, 0:4] = y_low[z, 12:16]
        m[p, 4:20] = m_own[z]
        m[p, 20:24] = y_high[z, 12:16]
        k[p, 0:8] = y_low[z, 16:24]
        k[p, 8:24] = k_own[z]
        k[p, 24:32] = y_high[z, 16:24]

    each((0, 16), own)
    place_planes(partner.at[1 - odd], 1 - odd, b, m, k)
    fine_part(odd, True, *refs)


def fine_far_kernel(place, cross, *refs):
    refs = refs[9:]
    b, u, k, m, message, co_out, first, k1, sums, tmp = refs
    odd = place[0] & 1
    place_planes(cross, odd, b, m, k)
    fine_part(odd, False, *refs)
    odd_lane = (lanes_of(8) & 1) != 0
    for z1 in range(4):
        message[16 + z1] = jnp.where(odd_lane, sums[z1 + 4], sums[z1])


def middle_part(odd, near, b1, u1, k1, t1, co_out, first, b2, k2, tmp):
    co = tuple(co_out.at[n] for n in range(5))
    even = 1 - odd
    if near:
        (c_low, c_count), (s_low, s_count) = (8 * even, 16), (1 + 8 * even, 14)
        (k_low, k_count), (d_low, d_count) = (4 * even, 8), (1 + 4 * even, 6)
    else:
        (c_low, c_count), (s_low, s_count) = (15 * odd, 9), (1 + 14 * odd, 8)
        (k_low, k_count), (d_low, d_count) = (8 * odd, 4), (1 + 6 * odd, 4)

    def fill(p):
        for ref, v in zip(co, coefficients(k1[p], None, k1[p + 1], 0.25, 2, None, t1[p])):
            ref[p] = v
        for c in range(3):
            first[c, p] = co[4][p] * b1[c, p]

    each((c_low, None, c_count), fill)
    sweep((s_low, None, s_count), b1, first, u1, k1, co, 2)

    def coarse_k(q2, s):
        k2[q2, 4:16] = block_mean(k1[2 * q2], k1[2 * q2 + 1], tmp.at[s], 2)
        k2[q2, 0:4] = jnp.zeros((4, 128), F32)

    span(k_low, k_count, coarse_k, 4)

    def down(q2, s):
        rests = [left_over(p, b1, u1, k1, co, 2)[1] for p in (2 * q2, 2 * q2 + 1)]
        for c in range(3):
            b2[c, q2, 4:16] = block_mean(rests[0][c], rests[1][c], tmp.at[3 * s + c], 2)
            b2[c, q2, 0:4] = jnp.zeros((4, 128), F32)

    span(d_low, d_count, down, 3 if near else 4)


def take(src, start, b1, k1, t1):
    odd_lane = (lanes_of(24) & 1) != 0
    for q in range(8):
        p = start + q
        v = src[q]
        b1[0, p] = jnp.where(odd_lane, lane_prev(v, 1), v)
        b1[1, p] = jnp.where(odd_lane, v, lane_next(v, 1))
        v = src[8 + q]
        b1[2, p] = jnp.where(odd_lane, lane_prev(v, 1), v)
        k1[p] = jnp.where(odd_lane, v, lane_next(v, 1))
    for q in range(4):
        v = src[16 + q]
        t1[start + q] = jnp.where(odd_lane, lane_prev(v, 1), v)
        t1[start + 4 + q] = jnp.where(odd_lane, v, lane_next(v, 1))


def middle_near_kernel(place, own, partner, *refs):
    b1, u1, k1, t1 = refs[:4]
    odd = place[0] & 1
    take(own, 8, b1, k1, t1)
    take(partner.at[1 - odd], 16 * (1 - odd), b1, k1, t1)
    k1[24] = jnp.zeros((24, 128), F32)
    middle_part(odd, True, *refs)


def middle_far_kernel(place, cross, *refs):
    refs = refs[8:]
    b1, u1, k1, t1, co_out, first, b2, k2 = refs[:8]
    u2b, packed, co2_out, u2a, tmp = refs[8:]
    odd = place[0] & 1
    take(cross, 16 * odd, b1, k1, t1)
    middle_part(odd, False, b1, u1, k1, t1, co_out, first, b2, k2, tmp)

    co2 = tuple(co2_out.at[n] for n in range(5))
    fill_coefficients(k2, co2, (1, 11), 0.0625, 4)
    co2[2][0] = (0.5 * 0.0625) * (k2[0] + k2[1])
    first_sweep((1, 11), b2, u2a, co2[4])
    sweep((2, 10), b2, u2a, u2b, k2, co2, 4)
    j = place[0] // 2
    lane = lanes_of(8)
    group = lane & 7
    pack = jnp.zeros((8, 128), F32)
    for zz in range(2):
        rests = [left_over(p, b2, u2b, k2, co2, 4)[1] for p in (4 + 2 * zz, 5 + 2 * zz)]
        parts = [block_mean(rests[0][c], rests[1][c], tmp.at[4 * zz + c], 4) for c in range(3)]
        parts.append(block_mean(k2[4 + 2 * zz], k2[5 + 2 * zz], tmp.at[4 * zz + 3], 4))
        for a in range(4):
            pack = jnp.where(group == ((j + 2 * a + zz) & 7), parts[a], pack)
    quad = lane & 3
    low, high = tmp.at[8], tmp.at[9]
    low[0:2] = pack[4:6]
    high[0:2] = pack[4:6]
    for c in range(3):
        v = u2b[c, 7, 8:16]
        for zz in (2, 1, 0):
            v = jnp.where(quad == zz, u2b[c, 4 + zz, 8:16], v)
        low[2 + 2 * c : 4 + 2 * c] = v[2:4]
        high[2 + 2 * c : 4 + 2 * c] = v[0:2]
    to_low, to_high = low[0:8], high[0:8]
    for peer in range(COL):
        packed[peer] = jnp.where(place[1] < peer, to_high, to_low)


def window_kernel(place, received, u2, out, tmp):
    c, d = place[1], place[0]
    for q in range(11):
        peer = c - 5 + q
        inside = jnp.logical_and(peer >= 0, peer < COL).astype(F32)
        tmp[2 * q : 2 * q + 2] = inside * received[jnp.clip(peer, 0, COL - 1), 0:2]
    for comp in range(3):
        for q, peer in ((0, c - 1), (1, c + 1)):
            inside = jnp.logical_and(peer >= 0, peer < COL).astype(F32)
            part = received[jnp.clip(peer, 0, COL - 1), 2 + 2 * comp : 4 + 2 * comp]
            base = 24 + 4 * comp + 2 * q
            tmp[base : base + 2] = inside * part
    quad = lanes_of(4) & 3
    tmp[22:24] = jnp.zeros((2, 128), F32)

    def inner(near):
        for comp in range(3):
            a = [u2[comp, 4 + near + f, 6:10] for f in range(2)]
            b = [u2[comp, 4 + near + f, 10:14] for f in range(2)]
            v = jnp.where(quad == 0, a[0], jnp.where(quad == 1, a[1], jnp.where(quad == 2, b[0], b[1])))
            tmp[36 + 4 * comp : 40 + 4 * comp] = v
        return tmp[...]

    to_high = inner(0)
    to_low = inner(2)
    for q in range(SLAB // 2):
        out[q] = jnp.where(q + 1 - (d & 1) > d // 2, to_high, to_low)


def upper_kernel(place, received, u2, b2, k2, co2, b1, u1, k1, co1, b0, u0, k0, m0, co0,
                 field, residual,
                 b3, k3, co3, u3a, u3b, u2a, u2b, u1a, u1b, u0a, u0b, tmp):
    d = place[0]
    lane = lanes_of(24)
    group = lane & 7

    def unpack(a, carry):
        mixes = [jnp.zeros((24, 128), F32)] * 8
        for j in range(8):
            v = received[a, j, 0:24]
            for r in range(8):
                mixes[r] = jnp.where(group == ((j + r) & 7), v, mixes[r])
        for r in range(8):
            mix = mixes[r]
            if r:
                mix = jnp.where(group < 8 - r, lane_next(mix, r), lane_prev(mix, 8 - r))
            arr, plane = r // 2, 2 * a + r % 2
            if arr < 3:
                b3[arr, plane] = mix
            else:
                k3[plane] = mix
        return carry

    lax.fori_loop(0, 2, unpack, 0)

    def above(v_of, i):
        return v_of(i + 1) if i < 3 else jnp.where(group < 7, lane_next(v_of(0), 1), 0.0)

    def below(v_of, i):
        return v_of(i - 1) if i > 0 else jnp.where(group > 0, lane_prev(v_of(3), 1), 0.0)

    cx3, cy3, cz3, e3, w3 = (co3.at[n] for n in range(5))
    for i in range(4):
        cx, cy, cz, e, w = coefficients(
            k3[i], below(lambda q: k3[q], i), above(lambda q: k3[q], i), 1.0 / 64.0, 8, None
        )
        cx3[i] = cx
        cy3[i] = cy
        cz3[i] = cz
        e3[i] = e
        w3[i] = w
        for c in range(3):
            u3a[c, i] = w * b3[c, i]

    def coarse(src, dst):
        for i in range(4):
            u = [src[c, i] for c in range(3)]
            lo = [below(lambda q: src[c, q], i) for c in range(3)]
            hi = [above(lambda q: src[c, q], i) for c in range(3)]
            b = [b3[c, i] for c in range(3)]
            cz_lo = below(lambda q: cz3[q], i)
            rest = remainder(b, u, lo, hi, k3[i], cx3[i], cy3[i], cz3[i], cz_lo, e3[i], 8)
            for c in range(3):
                dst[c, i] = u[c] + w3[i] * rest[c]

    def two(t, carry):
        coarse(u3a, u3b)
        coarse(u3b, u3a)
        return carry

    lax.fori_loop(0, 3, two, 0)
    coarse(u3a, u3b)

    c2 = tuple(co2.at[n] for n in range(5))
    lane8 = lanes_of(8)
    lane12 = lanes_of(12)

    def outer(g, carry):
        peer = d - 1 + g
        inside = jnp.logical_and(peer >= 0, peer < SLAB)
        peer = jnp.clip(peer, 0, SLAB - 1)
        rows = received[peer & 1, peer // 2, 24:36]
        for zz in range(4):
            pick = jnp.logical_and((lane12 & 3) == zz, inside)
            v = spread(jnp.where(pick, rows, 0.0), lane12, 4)
            for c in range(3):
                u2a[c, 4 * g + zz, 0:4] = jnp.zeros((4, 128), F32)
                u2a[c, 4 * g + zz, 4:6] = v[4 * c : 4 * c + 2]
                u2a[c, 4 * g + zz, 14:16] = v[4 * c + 2 : 4 * c + 4]
        return carry

    lax.fori_loop(0, 3, outer, 0)

    def middle(q2, _):
        for c in range(3):
            u2a[c, q2, 6:14] = u2[c, q2, 6:14]

    loop(2, 10, middle, 4)

    def far(g, carry):
        peer = d - 1 + 2 * g
        inside = jnp.logical_and(peer >= 0, peer < SLAB)
        peer = jnp.clip(peer, 0, SLAB - 1)
        rows = received[peer & 1, peer // 2, 36:48]
        for f in range(2):
            for half in range(2):
                pick = jnp.logical_and((lane12 & 3) == 2 * half + f, inside)
                v = spread(jnp.where(pick, rows, 0.0), lane12, 4)
                for c in range(3):
                    u2a[c, 10 * g + f, 6 + 4 * half : 10 + 4 * half] = v[4 * c : 4 * c + 4]
        return carry

    lax.fori_loop(0, 2, far, 0)

    def add_coarse(t, s):
        z = 2 * d - 2 + t
        i = (z + 32) & 3
        j = z >> 2
        for c in range(3):
            v = jnp.where((lane8 & 7) == j, u3b[c, i, 8:16], 0.0)
            double_rows(spread(v, lane8, 8), tmp.at[3 * s + c])
            for q2 in (2 * t, 2 * t + 1):
                u2a[c, q2, 4:16] = u2a[c, q2, 4:16] + tmp[3 * s + c, 0:12]

    loop(0, 6, add_coarse, 3)
    sweep((1, 11), b2, u2a, u2b, k2, c2, 4)
    sweep((2, 10), b2, u2b, u2a, k2, c2, 4)

    c1 = tuple(co1.at[n] for n in range(5))

    def add_middle(q2, s):
        for c in range(3):
            double_rows(u2a[c, q2, 6:14], tmp.at[3 * s + c])
            more = tmp[3 * s + c, 0:16]
            for p in (2 * q2 - 4, 2 * q2 - 3):
                u1a[c, p] = u1[c, p + 4, 4:20] + more

    loop(2, 10, add_middle, 4)
    sweep((1, 15), b1, u1a, u1b, k1, c1, 2, part=(4, slice(4, 20)))
    sweep((2, 14), b1, u1b, u1a, k1, c1, 2, part=(4, slice(4, 20)))

    c0 = tuple(co0.at[n] for n in range(5))
    def add_fine(p1, s):
        for c in range(3):
            double_rows(u1a[c, p1], tmp.at[3 * s + c])
            more = tmp[3 * s + c, 4:28]
            for p in (2 * p1 - 3, 2 * p1 - 2):
                u0a[c, p] = u0[c, p] + m0[p] * more

    loop(2, 14, add_fine, 4)
    sweep((3, 23), b0, u0a, u0b, k0, c0, 1, FINE)
    sweep((4, 22), b0, u0b, u0a, k0, c0, 1, FINE)

    def last(z):
        p = z + 5
        u, rest = left_over(p, b0, u0a, k0, c0, 1, FINE)
        for c in range(3):
            field[c, z] = u[c][4:20]
            residual[c, z] = (m0[p] * rest[c])[4:20]

    each((0, 16), last)


def struct(*shape):
    return jax.ShapeDtypeStruct(shape, F32)


def call(kernel, name, outs, scratch, *args, smem=0, alias=None, flops=0):
    vmem = pl.BlockSpec(memory_space=pltpu.VMEM)
    specs = [pl.BlockSpec(memory_space=pltpu.SMEM)] * smem
    return pl.pallas_call(
        kernel,
        name=name,
        out_shape=outs,
        in_specs=specs + [vmem] * (len(args) - len(specs)),
        out_specs=jax.tree.map(lambda _: vmem, outs),
        scratch_shapes=[pltpu.VMEM(s, F32) for s in scratch],
        input_output_aliases=alias or {},
        cost_estimate=pl.CostEstimate(flops=flops, bytes_accessed=flops, transcendentals=0) if flops else None,
        compiler_params=pltpu.CompilerParams(vmem_limit_bytes=40 * 1024 * 1024),
    )(*args)


def shift(block, axis, count, by):
    pairs = [(i, i + by) for i in range(count) if 0 <= i + by < count]
    return lax.ppermute(block, axis, pairs)


def slab_neighbours(to_partner, to_cross):
    pairs = []
    for i in range(1, SLAB - 1, 2):
        pairs += [(i, i + 1), (i + 1, i)]
    cross = lax.ppermute(to_cross, "slab", pairs)
    groups = [[i, i + 1] for i in range(0, SLAB, 2)]
    return lax.all_gather(to_partner, "slab", axis_index_groups=groups), cross


def on_device(load, density, moduli, fixed):
    place = jnp.stack([lax.axis_index("slab"), lax.axis_index("col")]).astype(jnp.int32)
    own = struct(16, 16, 128)
    raw = jnp.concatenate([load, density[None].astype(F32), fixed[None].astype(F32)], axis=0)
    k, m, low, high = call(
        prep_kernel, "prep", (own, own, struct(16, 24, 128), struct(16, 24, 128)), [], moduli, raw, smem=1
    )
    y_low = shift(high, "col", COL, 1)
    y_high = shift(low, "col", COL, -1)
    to_partner, to_cross = call(
        planes_kernel, "planes", (struct(544, 128), struct(544, 128)), [],
        place, raw, k, m, y_low, y_high, smem=1,
    )
    partner, cross = slab_neighbours(to_partner, to_cross)
    part0, full0, full0v = (26, 24, 128), (26, 32, 128), (3, 26, 24, 128)
    kept = (struct(*full0v), struct(*full0v), struct(*full0), struct(*part0), struct(20, 8, 128),
            struct(5, *part0), struct(*full0v), struct(10, 16, 128), struct(8, 8, 128))
    rows = [(16, 48, 128)]
    near = call(
        fine_near_kernel, "fine_near", kept, rows, place, raw, k, m, y_low, y_high, partner,
        smem=1, flops=8_000_000,
    )
    b0, u0, k0, m0, message, co0, *_ = call(
        fine_far_kernel, "fine_far", kept, rows, place, cross, *near,
        smem=1, alias={2 + n: n for n in range(len(kept))},
    )
    y_low = shift(message, "col", COL, 1)
    y_high = shift(message, "col", COL, -1)
    wide = jnp.concatenate([y_low, message, y_high], axis=1)
    partner, cross = slab_neighbours(wide, wide)
    full1, full1v, more1 = (24, 24, 128), (3, 24, 24, 128), (25, 24, 128)
    part1v = (3, 16, 16, 128)
    full2, full2v = (12, 16, 128), (3, 12, 16, 128)
    kept = (struct(*full1v), struct(*full1v), struct(*more1), struct(*full1), struct(5, *full1), struct(*full1v),
            struct(*full2v), struct(*full2))
    near = call(
        middle_near_kernel, "middle_near", kept, rows, place, wide, partner, smem=1, flops=8_000_000
    )
    outs = call(
        middle_far_kernel, "middle_far",
        kept + (struct(*full2v), struct(COL, 8, 128), struct(5, *full2)),
        [full2v] + rows, place, cross, *near,
        smem=1, alias={2 + n: n for n in range(len(kept))},
    )
    b1, u1, k1, _, co1, _, b2, k2, u2, packed, co2 = outs
    received = lax.all_to_all(packed, "col", 0, 0)
    window = call(window_kernel, "window", struct(SLAB // 2, 48, 128), [(48, 128)], place, received, u2, smem=1)
    groups = [list(range(par, SLAB, 2)) for par in range(2)]
    received = lax.all_to_all(window, "slab", 0, 0, axis_index_groups=groups)
    received = lax.all_gather(received, "slab", axis_index_groups=[[i, i + 1] for i in range(0, SLAB, 2)])
    full3, full3v = (4, 24, 128), (3, 4, 24, 128)
    return call(
        upper_kernel, "upper",
        (struct(3, 16, 16, 128), struct(3, 16, 16, 128)),
        [full3v, full3, (5,) + full3, full3v, full3v, full2v, full2v,
         part1v, part1v, full0v, full0v, (16, 48, 128)],
        place, received, u2, b2, k2, co2, b1, u1, k1, co1, b0, u0, k0, m0, co0, smem=1,
    )


def solution(mesh):
    placed = (P(None, "slab", "col", None), P("slab", "col", None), P(), P("slab", "col", None))
    return jax.shard_map(
        on_device,
        mesh=mesh,
        in_specs=placed,
        out_specs=(P(None, "slab", "col", None), P(None, "slab", "col", None)),
        check_vma=False,
    )
```
